256 devices in a mesh: ctx: 16 (over x, z_lo), ch: 16 (over y, z_hi, core).
Axes of the slice: x: 4, y: 4, z: 8 (z_hi: 2, z_lo: 4; z = z_hi * 4 + z_lo), core: 2. Of those that a mesh axis runs over, the one named last changes fastest.
Arguments:
- features: bfloat16 [3, 2048, 8192], P(None, 'ch', 'ctx'), may hold values from -6 to 6
- short_taps: float32 [3, 2048, 3], P(None, 'ch'), may hold values from -3.5 to 3.5
- decay: float32 [2048, 16], P(('ch', 'ctx')), may hold values from 6.1035156e-05 to 0.05
- residue: float32 [2048, 16], P(('ch', 'ctx')), may hold values from -0.32 to 0.32
- skip_bias: float32 [2048], P('ch'), may hold values from -4 to 4
- out_weight: bfloat16 [2048, 2048], P('ch'), may hold values from -0.125 to 0.125
Outputs:
- output: bfloat16 [2048, 8192], P('ch', 'ctx')
The draws below stay inside these ranges and needn't reach their ends.
All inputs are finite; a program needn't handle non-finite values.
Results may differ from the reference program's by a relative error of at most 0.013.
Values may be sent and summed in bfloat16 or wider, within the bound.
No kernel may reach another device: no remote copies, remote signals or barrier semaphores. Data moves between devices by JAX's collectives and lax.ppermute only.
A program may use at most 64 MiB of HBM per device.

```python
import math
import jax
import jax.numpy as jnp
from jax import lax

D = 2048
MODES = 16
TAPS = 3
SEQ = 8192


def log_rates(key, slow_share):
    choose = jax.random.uniform(jax.random.fold_in(key, 11), (D, MODES))
    spread = jax.random.uniform(jax.random.fold_in(key, 12), (D, MODES))
    slow_low = math.log(0.5 / SEQ)
    slow_high = math.log(2.3 / SEQ)
    fast_high = math.log(0.05)
    slow_part = slow_low + spread * (slow_high - slow_low)
    fast_part = slow_high + spread * (fast_high - slow_high)
    return jnp.where(choose < slow_share, slow_part, fast_part)


def draw_decay(key, part):
    share = 0.35
    rates = jnp.exp(log_rates(key, share))
    return rates.astype(jnp.float32)


def draw_residue(key, part):
    rates = jnp.exp(log_rates(key, 0.35))
    key = jax.random.fold_in(key, 5)
    signs = jnp.clip(jax.random.normal(key, (D, MODES)), -4.0, 4.0)
    return (signs * jnp.sqrt(2.0 * rates / MODES)).astype(jnp.float32)


def steps_of(rng, extent, split, least, high):
    gain, own = 1.0, jax.random.fold_in(rng, 6)
    for axis_at, parts in split:
        heights = jnp.exp(jax.random.uniform(jax.random.fold_in(own, axis_at), (parts,), jnp.float32, least / len(split), high / len(split)))
        gain = gain * jnp.repeat(heights, extent[axis_at] // parts).reshape([-1 if axis == axis_at else 1 for axis in range(len(extent))])
    return gain


def normal_values(own_key, extent, scale, bound, cuts=(), kind=jnp.bfloat16):
    values = jax.random.normal(own_key, extent, jnp.float32) * scale
    if len(cuts) > 0:
        values = steps_of(own_key, extent, cuts, -0.22, 0.18) * values
    return jnp.clip(values, min=-bound, max=bound).astype(kind)


def setup_inputs(seed: int = 0) -> dict:
    splits = jax.random.split(jax.random.key(seed), 7)
    return {
        "features": normal_values(splits[0], (3, D, SEQ), 1.0, 6.0, ((1, 16), (2, 16))),
        "short_taps": normal_values(splits[1], (3, D, TAPS), TAPS ** -0.5, 3.5, ((1, 16),), jnp.float32),
        "decay": draw_decay(jax.random.fold_in(splits[6], 71), 0),
        "residue": draw_residue(jax.random.fold_in(splits[6], 71), 0),
        "skip_bias": normal_values(splits[4], (D,), 1.0, 4.0, ((0, 16),), jnp.float32),
        "out_weight": normal_values(splits[5], (D, D), D ** -0.5, 0.125, ((0, 16),)),
    }


def short_filter(features, short_taps):
    tap_count = short_taps.shape[2]
    values = features.astype(jnp.float32)
    length = values.shape[2]
    padded = jnp.pad(values, ((0, 0), (0, 0), (tap_count - 1, 0)))
    summed = jnp.zeros(values.shape, jnp.float32)
    for offset in range(tap_count):
        start_at = tap_count - 1 - offset
        summed = summed + short_taps[:, :, offset:offset + 1] * padded[:, :, start_at:start_at + length]
    return summed


def block_convolve(pieces):
    mixed_block, decay_block, residue_block = pieces
    moments = jnp.arange(SEQ, dtype=jnp.float32)

    def add_mode(mode_id, summed):
        rate_now = lax.dynamic_index_in_dim(decay_block, mode_id, 1, keepdims=False)
        weight = lax.dynamic_index_in_dim(residue_block, mode_id, 1, keepdims=False)
        return summed + weight[:, None] * jnp.exp(-rate_now[:, None] * moments[None, :])

    impulse = lax.fori_loop(0, MODES, add_mode, jnp.zeros((decay_block.shape[0], SEQ), jnp.float32))
    impulse_spec = jnp.fft.rfft(impulse, n=2 * SEQ, axis=1)
    mixed_spec = jnp.fft.rfft(mixed_block.astype(jnp.float32), n=2 * SEQ, axis=1)
    return jnp.fft.irfft(impulse_spec * mixed_spec, n=2 * SEQ, axis=1)[:, :SEQ].astype(jnp.float32)


def reference(features, short_taps, decay, residue, skip_bias, out_weight):
    filtered = short_filter(features, short_taps)
    mixed = (filtered[1] * filtered[2]).astype(jnp.bfloat16)
    groups = D // 128
    convolved = lax.map(block_convolve, (mixed.reshape(groups, 128, SEQ), decay.reshape(groups, 128, MODES), residue.reshape(groups, 128, MODES)))
    convolved = convolved.reshape(D, SEQ)
    gated = (filtered[0] * (convolved + skip_bias[:, None] * mixed.astype(jnp.float32))).astype(jnp.bfloat16)
    return jnp.dot(out_weight, gated, preferred_element_type=jnp.float32).astype(jnp.bfloat16)
```

```python
import functools

import jax
import jax.numpy as jnp
from jax import lax
from jax.experimental import pallas as pl
from jax.experimental.pallas import tpu as pltpu
from jax.sharding import Mesh
from jax.sharding import PartitionSpec as P

CTX = ("x", "zl")
CH = ("y", "zh", "c")
LANES = 128
f32 = jnp.float32
bf16 = jnp.bfloat16


def shift(value, axis, steps):
    count = lax.axis_size(axis)
    return lax.ppermute(value, axis, [(i, (i + steps) % count) for i in range(count)])


def split_store(ref, index, value):
    high = value.astype(bf16)
    ref[(0,) + index] = high
    ref[(1,) + index] = (value - high.astype(f32)).astype(bf16)


def prep_body(decay, residue, decay_row, residue_row, bias, toeplitz, enter, leave, powers):
    owned, modes = decay.shape
    lane = lax.broadcasted_iota(jnp.int32, (owned, LANES), 1)
    moment = lane.astype(f32)
    impulse = jnp.where(lane == 0, bias[...], 0.0)
    for n in range(modes):
        impulse = impulse + residue[:, n : n + 1] * jnp.exp(-decay[:, n : n + 1] * moment)
    row = lax.broadcasted_iota(jnp.int32, (LANES, LANES), 0)
    col = lax.broadcasted_iota(jnp.int32, (LANES, LANES), 1)
    rate = decay_row[...]
    into = jnp.exp(-rate * (LANES - 1 - row).astype(f32))
    out_of = jnp.transpose(residue_row[...] * jnp.exp(-rate * (row + 1).astype(f32)))
    for c in range(owned):
        spread = jnp.broadcast_to(impulse[c : c + 1, :], (LANES, LANES))
        rolled = pltpu.roll(spread, 0, 1, stride=1, stride_axis=0)
        split_store(toeplitz, (c,), jnp.where(col >= row, rolled, 0.0))
        part = pl.ds(c * LANES, LANES)
        split_store(enter, (part, slice(None)), jnp.where(col // modes == c, into, 0.0))
        split_store(leave, (slice(None), part), jnp.where(row // modes == c, out_of, 0.0))
    for i in range(8):
        powers[i : i + 1, :] = jnp.exp(-rate * float(LANES << i))


def dot(a, b):
    return jnp.dot(a, b, preferred_element_type=f32)


def conv_body(kv, taps, toeplitz, enter, leave, powers, out, mixed_buf, conv_buf):
    shards, _, owned, tokens = kv.shape
    per = tokens // LANES
    blocks = shards * per
    lane = lax.broadcasted_iota(jnp.int32, (owned, LANES), 1)
    weights = [[taps[s, :, j : j + 1] for j in range(3)] for s in range(2)]
    zero = jnp.zeros((owned, LANES), f32)
    last = [(zero, zero), (zero, zero)]
    for b in range(blocks):
        k, j = divmod(b, per)
        product = None
        for s in range(2):
            now = kv[k, s, :, j * LANES : (j + 1) * LANES].astype(f32)
            one, two = pltpu.roll(now, 1, 1), pltpu.roll(now, 2, 1)
            w = weights[s]
            value = (
                w[0] * now
                + w[1] * jnp.where(lane < 1, last[s][0], one)
                + w[2] * jnp.where(lane < 2, last[s][1], two)
            )
            last[s] = (one, two)
            product = value if product is None else product * value
        mixed_buf[b] = product.astype(bf16).astype(f32)
    mixed = [mixed_buf[:, c, :].astype(bf16) for c in range(owned)]
    whole = jnp.concatenate(mixed, axis=1)
    state = dot(whole, enter[0]) + dot(whole, enter[1])
    row = lax.broadcasted_iota(jnp.int32, (blocks, LANES), 0)
    step, i = 1, 0
    while step < blocks:
        moved = jnp.where(row < step, 0.0, pltpu.roll(state, step, 0))
        state = state + powers[i : i + 1, :] * moved
        step, i = step * 2, i + 1
    state = jnp.where(row < 1, 0.0, pltpu.roll(state, 1, 0))
    high = state.astype(bf16)
    low = (state - high.astype(f32)).astype(bf16)
    for c in range(owned):
        part = pl.ds(c * LANES, LANES)
        value = dot(mixed[c], toeplitz[0, c]) + dot(mixed[c], toeplitz[1, c])
        value = value + dot(high, leave[0, :, part]) + dot(high, leave[1, :, part])
        conv_buf[:, c, :] = value + dot(low, leave[0, :, part])
    for b in range(blocks):
        k, j = divmod(b, per)
        value = conv_buf[b].astype(bf16)
        for h in range(out.shape[0]):
            out[h, k, :, j * LANES : (j + 1) * LANES] = value


def merge_body(y_unused, own, other, core, weight, out0, out1, out2, out3, gathered):
    half = own.shape[0] // 2
    me = core[0]
    for h in range(2):
        at = pl.multiple_of(h * 2 * half + me * half, half)
        gathered[pl.ds(at, half), :] = own[h * half : (h + 1) * half, :]
        at = pl.multiple_of(h * 2 * half + (1 - me) * half, half)
        gathered[pl.ds(at, half), :] = other[h * half : (h + 1) * half, :]


def vmem(count):
    return [pl.BlockSpec(memory_space=pltpu.VMEM)] * count


def convolve(kv, taps, decay, residue, bias, copies):
    owned, modes = decay.shape
    shards, _, _, tokens = kv.shape
    wide = owned * LANES
    mats = pl.pallas_call(
        prep_body,
        out_shape=(
            jax.ShapeDtypeStruct((2, owned, LANES, LANES), bf16),
            jax.ShapeDtypeStruct((2, wide, LANES), bf16),
            jax.ShapeDtypeStruct((2, LANES, wide), bf16),
            jax.ShapeDtypeStruct((8, LANES), f32),
        ),
        in_specs=vmem(5),
        out_specs=tuple(vmem(4)),
        cost_estimate=pl.CostEstimate(flops=2000000, bytes_accessed=1600000, transcendentals=70000),
        name="prep",
    )(decay, residue, decay.reshape(1, wide // modes * modes // LANES * modes), residue.reshape(1, owned * modes), bias)
    return mats


def conv_call(kv, taps, mats, copies):
    shards, _, owned, tokens = kv.shape
    blocks = shards * tokens // LANES
    return pl.pallas_call(
        conv_body,
        out_shape=jax.ShapeDtypeStruct((copies, shards, owned, tokens), bf16),
        in_specs=vmem(6),
        out_specs=vmem(1)[0],
        scratch_shapes=[pltpu.VMEM((blocks, owned, LANES), f32)] * 2,
        cost_estimate=pl.CostEstimate(flops=100000000, bytes_accessed=2500000, transcendentals=0),
        name="conv",
    )(kv, taps, *mats)


def merge_kernel(own, other, core, w0, w1, w2, w3, o0, o1, o2, o3, gathered):
    half = own.shape[0] // 2
    me = core[0]
    for h in range(2):
        at = pl.multiple_of((2 * h + me) * half, half)
        gathered[pl.ds(at, half), :] = own[h * half : (h + 1) * half, :]
        at = pl.multiple_of((2 * h + 1 - me) * half, half)
        gathered[pl.ds(at, half), :] = other[h * half : (h + 1) * half, :]
    for w, o in ((w2, o2), (w1, o1), (w3, o3), (w0, o0)):
        o[...] = dot(w[...], gathered[...]).astype(o.dtype)


def local(features, short_taps, decay, residue, skip_bias, out_weight):
    _, channels, tokens = features.shape
    shards = lax.axis_size("x") * lax.axis_size("zl")
    owned, modes = decay.shape
    ctx = lax.axis_index("x") * lax.axis_size("zl") + lax.axis_index("zl")
    y, zh, core = (lax.axis_index(a) for a in CH)
    ys = lax.axis_size("y")
    cols = out_weight.shape[1] // ys

    sent = features[1:].reshape(2, shards, owned, tokens).transpose(1, 0, 2, 3)
    kv = lax.all_to_all(sent, CTX, 0, 0, tiled=True)

    weights = [lax.dynamic_slice_in_dim(out_weight, y * cols, cols, 1)]
    for d in range(1, ys):
        block = lax.dynamic_slice_in_dim(out_weight, (y + ys - d) % ys * cols, cols, 1)
        weights.append(shift(block, "y", -d))

    total = shards
    rim = lax.ppermute(features[0, :, tokens - 2 :], CTX, [(i, i + 1) for i in range(total - 1)])
    longer = jnp.concatenate([rim, features[0]], axis=1).astype(f32)
    query = sum(
        short_taps[0, :, j : j + 1] * longer[:, 2 - j : 2 - j + tokens] for j in range(3)
    ).astype(bf16)
    query_other = shift(query, "zh", 1)

    taps = lax.dynamic_slice_in_dim(short_taps[1:], ctx * owned, owned, 1)
    bias = lax.dynamic_slice_in_dim(skip_bias, ctx * owned, owned, 0)[:, None]
    mats = pl.pallas_call(
        prep_body,
        out_shape=(
            jax.ShapeDtypeStruct((2, owned, LANES, LANES), bf16),
            jax.ShapeDtypeStruct((2, owned * LANES, LANES), bf16),
            jax.ShapeDtypeStruct((2, LANES, owned * LANES), bf16),
            jax.ShapeDtypeStruct((8, LANES), f32),
        ),
        in_specs=vmem(5),
        out_specs=tuple(vmem(4)),
        cost_estimate=pl.CostEstimate(flops=2000000, bytes_accessed=1600000, transcendentals=70000),
        name="prep",
    )(decay, residue, decay.reshape(1, -1), residue.reshape(1, -1), bias)
    conv = conv_call(kv, taps, mats, 2)
    conv = lax.all_to_all(
        conv.reshape(2 * shards, owned, tokens), ("zh",) + CTX, 0, 0, tiled=True
    ).reshape(2, channels, tokens)
    first = zh == 0
    both = jnp.stack([jnp.where(first, query, query_other), jnp.where(first, query_other, query)])
    gated = (both.astype(f32) * conv.astype(f32)).astype(bf16).reshape(2 * channels, tokens)
    gated_other = shift(gated, "c", 1)
    rows = out_weight.shape[0]
    parts = pl.pallas_call(
        merge_kernel,
        out_shape=(jax.ShapeDtypeStruct((rows, tokens), f32),)
        + (jax.ShapeDtypeStruct((rows, tokens), bf16),) * 3,
        in_specs=vmem(2) + [pl.BlockSpec(memory_space=pltpu.SMEM)] + vmem(4),
        out_specs=tuple(vmem(4)),
        scratch_shapes=[pltpu.VMEM((4 * channels, tokens), bf16)],
        cost_estimate=pl.CostEstimate(flops=300000000, bytes_accessed=2500000, transcendentals=0),
        name="merge",
    )(gated, gated_other, core.reshape(1), *weights)
    total = parts[0]
    for d in range(1, ys):
        total = total + shift(parts[d], "y", d).astype(f32)
    return total.astype(bf16)


def solution(mesh):
    split = Mesh(mesh.devices.reshape(4, 4, 4, 2, 2), CTX + CH)
    in_specs = (
        P(None, CH, CTX),
        P(None, CH, None),
        P(CH + CTX, None),
        P(CH + CTX, None),
        P(CH),
        P(CH, None),
    )
    return jax.shard_map(local, mesh=split, in_specs=in_specs, out_specs=P(CH, CTX), check_vma=False)
```

```python
import jax
import jax.numpy as jnp
from jax import lax
from jax.experimental import pallas as pl
from jax.experimental.pallas import tpu as pltpu
from jax.sharding import Mesh
from jax.sharding import PartitionSpec as P

CTX = ("x", "zl")
CH = ("y", "zh", "c")
GO = ("x", "zl")
BACK = ("x", "zl", "zh")
LANES = 128
TAPS = 3
f32 = jnp.float32
bf16 = jnp.bfloat16
in_vmem = pl.BlockSpec(memory_space=pltpu.VMEM)


def shift(value, axis, steps):
    count = lax.axis_size(axis)
    return lax.ppermute(value, axis, [(i, (i + steps) % count) for i in range(count)])


def place(order, k, h=0):
    at = {"x": k // 4, "zl": k % 4, "zh": h}
    size = {"x": 4, "zl": 4, "zh": 2}
    index = 0
    for axis in order:
        index = index * size[axis] + at[axis]
    return index


def near(value):
    return pltpu.with_memory_space_constraint(value, pltpu.VMEM)


def params(**kwargs):
    return pltpu.CompilerParams(vmem_limit_bytes=16 << 20, **kwargs)


def ctx_index():
    return lax.axis_index("x") * lax.axis_size("zl") + lax.axis_index("zl")


def split_store(ref, index, value):
    high = value.astype(bf16)
    ref[(0,) + index] = high
    ref[(1,) + index] = (value - high.astype(f32)).astype(bf16)


def pack_body(features_hbm, taps_hbm, sent, features, short_taps, sem):
    copies = [pltpu.make_async_copy(taps_hbm, short_taps, sem.at[3])]
    for s in range(3):
        copies.append(pltpu.make_async_copy(features_hbm.at[s], features.at[s], sem.at[s]))
    for copy in copies:
        copy.start()
    for copy in copies:
        copy.wait()
    _, channels, tokens = features.shape
    shards, owned, _ = sent.shape
    per = tokens // LANES
    rows = [short_taps[s] for s in range(3)]
    filler = jnp.zeros((LANES - 3 * TAPS, channels), f32)
    columns = jnp.transpose(jnp.concatenate(rows + [filler], axis=0))
    lane = lax.broadcasted_iota(jnp.int32, (owned, LANES), 1)
    zero = jnp.zeros((owned, LANES), f32)
    for k in range(shards):
        at = slice(k * owned, (k + 1) * owned)
        rims = zero
        value = [[], [], []]
        for s in range(3):
            w = [
                jnp.broadcast_to(columns[at, i : i + 1], (owned, LANES))
                for i in range(s * TAPS, (s + 1) * TAPS)
            ]
            last = (zero, zero)
            for j in range(per):
                now = features[s, at, j * LANES : (j + 1) * LANES].astype(f32)
                one, two = pltpu.roll(now, 1, 1), pltpu.roll(now, 2, 1)
                value[s].append(
                    w[0] * now
                    + w[1] * jnp.where(lane < 1, last[0], one)
                    + w[2] * jnp.where(lane < 2, last[1], two)
                )
                last = (one, two)
                if j == 0:
                    head = pltpu.roll(now, 4 * s, 1) if s else now
                    rims = jnp.where((lane == 4 * s) | (lane == 4 * s + 1), head, rims)
                if j == per - 1:
                    tail = pltpu.roll(now, 4 * s + 4, 1)
                    rims = jnp.where((lane == 4 * s + 2) | (lane == 4 * s + 3), tail, rims)
        for j in range(per):
            part = slice(j * LANES, (j + 1) * LANES)
            sent[place(GO, k), :, part] = (value[1][j] * value[2][j]).astype(bf16)
            part = slice(tokens + j * LANES, tokens + (j + 1) * LANES)
            sent[place(GO, k), :, part] = value[0][j].astype(bf16)
        sent[place(GO, k), :, 2 * tokens :] = rims.astype(bf16)


def prep_body(decay, residue, skip_bias, short_taps, toeplitz, enter, leave, powers, taps):
    owned, modes = decay.shape
    lane = lax.broadcasted_iota(jnp.int32, (owned, LANES), 1)
    sub = lax.broadcasted_iota(jnp.int32, (owned, LANES), 0)
    mine = lane == sub + ctx_index() * owned

    def own_column(values):
        picked = jnp.sum(jnp.where(mine, values, 0.0), axis=1, keepdims=True)
        return jnp.broadcast_to(picked, (owned, LANES))

    def as_row(values):
        tiled = jnp.concatenate([values] * owned, axis=1)
        return jnp.sum(jnp.where(lane // modes == sub, tiled, 0.0), axis=0, keepdims=True)

    for s in range(3):
        for j in range(TAPS):
            taps[s * TAPS + j] = own_column(short_taps[s, j : j + 1, :])
    moment = lane.astype(f32)
    impulse = jnp.where(lane == 0, own_column(skip_bias[...]), 0.0)
    rates, weights = decay[...], residue[...]
    for n in range(modes):
        impulse = impulse + weights[:, n : n + 1] * jnp.exp(-rates[:, n : n + 1] * moment)
    row = lax.broadcasted_iota(jnp.int32, (LANES, LANES), 0)
    col = lax.broadcasted_iota(jnp.int32, (LANES, LANES), 1)
    rate = as_row(rates)
    into = jnp.exp(-rate * (LANES - 1 - row).astype(f32))
    out_of = jnp.transpose(as_row(weights) * jnp.exp(-rate * (row + 1).astype(f32)))
    for c in range(owned):
        spread = jnp.broadcast_to(impulse[c : c + 1, :], (LANES, LANES))
        rolled = pltpu.roll(spread, 0, 1, stride=1, stride_axis=0)
        split_store(toeplitz, (c,), jnp.where(col >= row, rolled, 0.0))
        part = pl.ds(c * LANES, LANES)
        split_store(enter, (part, slice(None)), jnp.where(col // modes == c, into, 0.0))
        split_store(leave, (slice(None), part), jnp.where(row // modes == c, out_of, 0.0))
    for i in range(8):
        powers[i : i + 1, :] = jnp.exp(-rate * float(LANES << i))


def dot(a, b):
    return jnp.dot(a, b, preferred_element_type=f32)


def conv_body(held, taps, toeplitz, enter, leave, powers, w1, w2, w3, out, mixed_buf, query_buf, conv_buf):
    shards, owned, _ = held.shape
    tokens = out.shape[-1]
    per = tokens // LANES
    blocks = shards * per
    lane = lax.broadcasted_iota(jnp.int32, (owned, LANES), 1)
    weights = [
        jnp.where(lane < 4, taps[j], jnp.where(lane < 8, taps[TAPS + j], taps[2 * TAPS + j]))
        for j in range(TAPS)
    ]
    before = jnp.zeros((owned, LANES), f32)
    for k in range(shards):
        rims = held[place(GO, k), :, 2 * tokens :].astype(f32)
        older = pltpu.roll(before, LANES - 2, 1)
        middle = jnp.where(lane % 4 == 0, pltpu.roll(before, LANES - 3, 1), pltpu.roll(rims, 1, 1))
        head = weights[0] * rims + weights[1] * middle + weights[2] * older
        before = rims
        fixed = pltpu.roll(head, LANES - 4, 1) * pltpu.roll(head, LANES - 8, 1)
        for j in range(per):
            now = held[place(GO, k), :, j * LANES : (j + 1) * LANES].astype(f32)
            query = held[place(GO, k), :, tokens + j * LANES : tokens + (j + 1) * LANES].astype(f32)
            if j == 0:
                now = jnp.where(lane < 2, fixed.astype(bf16).astype(f32), now)
                query = jnp.where(lane < 2, head, query)
            mixed_buf[k * per + j] = now
            query_buf[k * per + j] = query
    mixed = [mixed_buf[:, c, :].astype(bf16) for c in range(owned)]
    whole = jnp.concatenate(mixed, axis=1)
    state = dot(whole, enter[0]) + dot(whole, enter[1])
    row = lax.broadcasted_iota(jnp.int32, (blocks, LANES), 0)
    step, i = 1, 0
    while step < blocks:
        moved = jnp.where(row < step, 0.0, pltpu.roll(state, step, 0))
        state = state + powers[i : i + 1, :] * moved
        step, i = step * 2, i + 1
    state = jnp.where(row < 1, 0.0, pltpu.roll(state, 1, 0))
    high = state.astype(bf16)
    low = (state - high.astype(f32)).astype(bf16)
    for c in range(owned):
        part = pl.ds(c * LANES, LANES)
        value = dot(mixed[c], toeplitz[0, c]) + dot(mixed[c], toeplitz[1, c])
        value = value + dot(high, leave[0, :, part]) + dot(high, leave[1, :, part])
        conv_buf[:, c, :] = value + dot(low, leave[0, :, part])
    for b in range(blocks):
        k, j = divmod(b, per)
        value = (query_buf[b] * conv_buf[b]).astype(bf16)
        for h in range(2):
            out[place(BACK, k, h), :, j * LANES : (j + 1) * LANES] = value


def settle_body(gated, w1, w2, w3, out):
    count, owned, _ = gated.shape
    for h in range(2):
        rows = [gated[place(BACK, k, h)] for k in range(count // 2)]
        out[pl.ds(h * (count // 2) * owned, count // 2 * owned), :] = jnp.concatenate(rows, axis=0)


def merge_body(core, own, other, w0, w1, w2, w3, o0, o1, o2, o3, gathered):
    half = own.shape[0] // 2
    me = core[0]
    for h in range(2):
        at = pl.multiple_of((2 * h + me) * half, half)
        gathered[pl.ds(at, half), :] = own[h * half : (h + 1) * half, :]
        at = pl.multiple_of((2 * h + 1 - me) * half, half)
        gathered[pl.ds(at, half), :] = other[h * half : (h + 1) * half, :]
    for w, o in ((w2, o2), (w1, o1), (w3, o3), (w0, o0)):
        o[...] = dot(w[...], gathered[...]).astype(o.dtype)


def add_body(o0, o1, o2, o3, out):
    total = o0[...] + o1[...].astype(f32) + o2[...].astype(f32) + o3[...].astype(f32)
    out[...] = total.astype(out.dtype)


def local(features, short_taps, decay, residue, skip_bias, out_weight):
    _, channels, tokens = features.shape
    shards = lax.axis_size("x") * lax.axis_size("zl")
    owned, modes = decay.shape
    blocks = shards * tokens // LANES
    y, zh, core = (lax.axis_index(a) for a in CH)

    columns = short_taps.transpose(0, 2, 1)
    sent = pl.pallas_call(
        pack_body,
        out_shape=pltpu.VMEM((shards, owned, 2 * tokens + LANES), bf16),
        in_specs=[pl.BlockSpec(memory_space=pltpu.HBM)] * 2,
        out_specs=in_vmem,
        scratch_shapes=[
            pltpu.VMEM(features.shape, bf16),
            pltpu.VMEM(columns.shape, f32),
            pltpu.SemaphoreType.DMA((4,)),
        ],
        compiler_params=params(),
        name="pack",
    )(*(pltpu.with_memory_space_constraint(a, pltpu.HBM) for a in (features, columns)))
    held = lax.all_to_all(sent, GO, 0, 0, tiled=True)

    ys = lax.axis_size("y")
    cols = out_weight.shape[1] // ys
    weights = [lax.dynamic_slice_in_dim(out_weight, y * cols, cols, 1)]
    for d in range(1, ys):
        block = lax.dynamic_slice_in_dim(out_weight, (y + ys - d) % ys * cols, cols, 1)
        weights.append(shift(block, "y", -d))

    mats = pl.pallas_call(
        prep_body,
        out_shape=(
            pltpu.VMEM((2, owned, LANES, LANES), bf16),
            pltpu.VMEM((2, owned * LANES, LANES), bf16),
            pltpu.VMEM((2, LANES, owned * LANES), bf16),
            pltpu.VMEM((8, LANES), f32),
            pltpu.VMEM((3 * TAPS, owned, LANES), f32),
        ),
        in_specs=[in_vmem] * 4,
        out_specs=(in_vmem,) * 5,
        cost_estimate=pl.CostEstimate(flops=2000000, bytes_accessed=1600000, transcendentals=70000),
        compiler_params=params(),
        name="prep",
    )(decay, residue, skip_bias.reshape(1, -1), columns)
    toeplitz, enter, leave, powers, taps = mats
    gated = pl.pallas_call(
        conv_body,
        out_shape=pltpu.VMEM((2 * shards, owned, tokens), bf16),
        in_specs=[in_vmem] * 6 + [pl.BlockSpec(memory_space=pl.ANY)] * 3,
        out_specs=in_vmem,
        scratch_shapes=[pltpu.VMEM((blocks, owned, LANES), f32)] * 3,
        cost_estimate=pl.CostEstimate(flops=100000000, bytes_accessed=2500000, transcendentals=0),
        compiler_params=params(),
        name="conv",
    )(*map(near, (held, taps, toeplitz, enter, leave, powers)), *weights[1:])
    gated = lax.all_to_all(gated, BACK, 0, 0, tiled=True)
    gated = pl.pallas_call(
        settle_body,
        out_shape=pltpu.VMEM((2 * channels, tokens), bf16),
        in_specs=[in_vmem] + [pl.BlockSpec(memory_space=pl.ANY)] * 3,
        out_specs=in_vmem,
        compiler_params=params(),
        name="settle",
    )(near(gated), *weights[1:])
    other = shift(gated, "c", 1)
    rows = out_weight.shape[0]
    parts = pl.pallas_call(
        merge_body,
        out_shape=(pltpu.VMEM((rows, tokens), f32),) + (pltpu.VMEM((rows, tokens), bf16),) * 3,
        in_specs=[pl.BlockSpec(memory_space=pltpu.SMEM)] + [in_vmem] * 6,
        out_specs=(in_vmem,) * 4,
        scratch_shapes=[pltpu.VMEM((4 * channels, tokens), bf16)],
        cost_estimate=pl.CostEstimate(flops=300000000, bytes_accessed=2500000, transcendentals=0),
        compiler_params=params(),
        name="merge",
    )(core.reshape(1), near(gated), near(other), *map(near, weights))
    arrived = [parts[0]] + [shift(parts[d], "y", d) for d in (1, 2, 3)]
    return pl.pallas_call(
        add_body,
        out_shape=jax.ShapeDtypeStruct((rows, tokens), bf16),
        in_specs=[in_vmem] * 4,
        out_specs=in_vmem,
        compiler_params=params(),
        name="add",
    )(*map(near, arrived))


def solution(mesh):
    split = Mesh(mesh.devices.reshape(4, 4, 4, 2, 2), CTX + CH)
    in_specs = (
        P(None, CH, CTX),
        P(None, CH, None),
        P(CH + CTX, None),
        P(CH + CTX, None),
        P(CH),
        P(CH, None),
    )
    return jax.shard_map(local, mesh=split, in_specs=in_specs, out_specs=P(CH, CTX), check_vma=False)
```

```python
import jax
import jax.numpy as jnp
from jax import lax
from jax.experimental import pallas as pl
from jax.experimental.pallas import tpu as pltpu
from jax.sharding import Mesh
from jax.sharding import PartitionSpec as P

CTX = ("x", "zl")
CH = ("y", "zh", "c")
GO = ("zl", "x")
BACK = ("zh", "zl", "x")
LANES = 128
TAPS = 3
ORDER = (2, 1, 3)
WAIT = 20_000_000_000
f32 = jnp.float32
bf16 = jnp.bfloat16
in_vmem = pl.BlockSpec(memory_space=pltpu.VMEM)


def shift(value, axis, steps):
    count = lax.axis_size(axis)
    return lax.ppermute(value, axis, [(i, (i + steps) % count) for i in range(count)])


def place(order, k, h=0):
    at = {"x": k // 4, "zl": k % 4, "zh": h}
    size = {"x": 4, "zl": 4, "zh": 2}
    index, count = 0, 1
    for axis in order:
        index = index * size[axis] + at[axis]
        count *= size[axis]
    return count - 1 - index


def exchange(value, order):
    backwards = [list(reversed(range(value.shape[0])))]
    return lax.all_to_all(value, order, 0, 0, axis_index_groups=backwards, tiled=True)


def near(value):
    return pltpu.with_memory_space_constraint(value, pltpu.VMEM)


def params(**kwargs):
    return pltpu.CompilerParams(vmem_limit_bytes=16 << 20, **kwargs)


def ctx_index():
    return lax.axis_index("x") * lax.axis_size("zl") + lax.axis_index("zl")


def split_store(ref, index, value):
    high = value.astype(bf16)
    ref[(0,) + index] = high
    ref[(1,) + index] = (value - high.astype(f32)).astype(bf16)


def pack_body(features_hbm, taps_hbm, sent, features, short_taps, sem):
    copies = [pltpu.make_async_copy(taps_hbm, short_taps, sem.at[3])]
    for s in range(3):
        copies.append(pltpu.make_async_copy(features_hbm.at[s], features.at[s], sem.at[s]))
    for copy in copies:
        copy.start()
    for copy in copies:
        copy.wait()
    _, channels, tokens = features.shape
    shards, owned, _ = sent.shape
    per = tokens // LANES
    rows = [short_taps[s] for s in range(3)]
    filler = jnp.zeros((LANES - 3 * TAPS, channels), f32)
    columns = jnp.transpose(jnp.concatenate(rows + [filler], axis=0))
    lane = lax.broadcasted_iota(jnp.int32, (owned, LANES), 1)
    zero = jnp.zeros((owned, LANES), f32)
    for k in range(shards):
        at = slice(k * owned, (k + 1) * owned)
        rims = zero
        value = [[], [], []]
        for s in range(3):
            w = [
                jnp.broadcast_to(columns[at, i : i + 1], (owned, LANES))
                for i in range(s * TAPS, (s + 1) * TAPS)
            ]
            last = (zero, zero)
            for j in range(per):
                now = features[s, at, j * LANES : (j + 1) * LANES].astype(f32)
                one, two = pltpu.roll(now, 1, 1), pltpu.roll(now, 2, 1)
                value[s].append(
                    w[0] * now
                    + w[1] * jnp.where(lane < 1, last[0], one)
                    + w[2] * jnp.where(lane < 2, last[1], two)
                )
                last = (one, two)
                if j == 0:
                    head = pltpu.roll(now, 4 * s, 1) if s else now
                    rims = jnp.where((lane == 4 * s) | (lane == 4 * s + 1), head, rims)
                if j == per - 1:
                    tail = pltpu.roll(now, 4 * s + 4, 1)
                    rims = jnp.where((lane == 4 * s + 2) | (lane == 4 * s + 3), tail, rims)
        for j in range(per):
            part = slice(j * LANES, (j + 1) * LANES)
            sent[place(GO, k), :, part] = (value[1][j] * value[2][j]).astype(bf16)
            part = slice(tokens + j * LANES, tokens + (j + 1) * LANES)
            sent[place(GO, k), :, part] = value[0][j].astype(bf16)
        sent[place(GO, k), :, 2 * tokens :] = rims.astype(bf16)


def prep_body(decay, residue, skip_bias, short_taps, toeplitz, enter, leave, powers, taps):
    owned, modes = decay.shape
    lane = lax.broadcasted_iota(jnp.int32, (owned, LANES), 1)
    sub = lax.broadcasted_iota(jnp.int32, (owned, LANES), 0)
    mine = lane == sub + ctx_index() * owned

    def own_column(values):
        picked = jnp.sum(jnp.where(mine, values, 0.0), axis=1, keepdims=True)
        return jnp.broadcast_to(picked, (owned, LANES))

    def as_row(values):
        tiled = jnp.concatenate([values] * owned, axis=1)
        return jnp.sum(jnp.where(lane // modes == sub, tiled, 0.0), axis=0, keepdims=True)

    for s in range(3):
        for j in range(TAPS):
            taps[s * TAPS + j] = own_column(short_taps[s, j : j + 1, :])
    moment = lane.astype(f32)
    impulse = jnp.where(lane == 0, own_column(skip_bias[...]), 0.0)
    rates, weights = decay[...], residue[...]
    for n in range(modes):
        impulse = impulse + weights[:, n : n + 1] * jnp.exp(-rates[:, n : n + 1] * moment)
    row = lax.broadcasted_iota(jnp.int32, (LANES, LANES), 0)
    col = lax.broadcasted_iota(jnp.int32, (LANES, LANES), 1)
    rate = as_row(rates)
    into = jnp.exp(-rate * (LANES - 1 - row).astype(f32))
    out_of = jnp.transpose(as_row(weights) * jnp.exp(-rate * (row + 1).astype(f32)))
    for c in range(owned):
        spread = jnp.broadcast_to(impulse[c : c + 1, :], (LANES, LANES))
        rolled = pltpu.roll(spread, 0, 1, stride=1, stride_axis=0)
        split_store(toeplitz, (c,), jnp.where(col >= row, rolled, 0.0))
        part = pl.ds(c * LANES, LANES)
        split_store(enter, (part, slice(None)), jnp.where(col // modes == c, into, 0.0))
        split_store(leave, (slice(None), part), jnp.where(row // modes == c, out_of, 0.0))
    for i in range(8):
        powers[i : i + 1, :] = jnp.exp(-rate * float(LANES << i))


def dot(a, b):
    return jnp.dot(a, b, preferred_element_type=f32)


def conv_body(held, taps, toeplitz, enter, leave, powers, out, mixed_buf, query_buf, conv_buf):
    shards, owned, _ = held.shape
    tokens = out.shape[-1]
    per = tokens // LANES
    blocks = shards * per
    lane = lax.broadcasted_iota(jnp.int32, (owned, LANES), 1)
    weights = [
        jnp.where(lane < 4, taps[j], jnp.where(lane < 8, taps[TAPS + j], taps[2 * TAPS + j]))
        for j in range(TAPS)
    ]
    before = jnp.zeros((owned, LANES), f32)
    for k in range(shards):
        rims = held[place(GO, k), :, 2 * tokens :].astype(f32)
        older = pltpu.roll(before, LANES - 2, 1)
        middle = jnp.where(lane % 4 == 0, pltpu.roll(before, LANES - 3, 1), pltpu.roll(rims, 1, 1))
        head = weights[0] * rims + weights[1] * middle + weights[2] * older
        before = rims
        fixed = pltpu.roll(head, LANES - 4, 1) * pltpu.roll(head, LANES - 8, 1)
        for j in range(per):
            now = held[place(GO, k), :, j * LANES : (j + 1) * LANES].astype(f32)
            query = held[place(GO, k), :, tokens + j * LANES : tokens + (j + 1) * LANES].astype(f32)
            if j == 0:
                now = jnp.where(lane < 2, fixed.astype(bf16).astype(f32), now)
                query = jnp.where(lane < 2, head, query)
            mixed_buf[k * per + j] = now
            query_buf[k * per + j] = query
    mixed = [mixed_buf[:, c, :].astype(bf16) for c in range(owned)]
    whole = jnp.concatenate(mixed, axis=1)
    state = dot(whole, enter[0]) + dot(whole, enter[1])
    row = lax.broadcasted_iota(jnp.int32, (blocks, LANES), 0)
    step, i = 1, 0
    while step < blocks:
        moved = jnp.where(row < step, 0.0, pltpu.roll(state, step, 0))
        state = state + powers[i : i + 1, :] * moved
        step, i = step * 2, i + 1
    state = jnp.where(row < 1, 0.0, pltpu.roll(state, 1, 0))
    high = state.astype(bf16)
    low = (state - high.astype(f32)).astype(bf16)
    for c in range(owned):
        part = pl.ds(c * LANES, LANES)
        value = dot(mixed[c], toeplitz[0, c]) + dot(mixed[c], toeplitz[1, c])
        value = value + dot(high, leave[0, :, part]) + dot(high, leave[1, :, part])
        conv_buf[:, c, :] = value + dot(low, leave[0, :, part])
    for b in range(blocks):
        k, j = divmod(b, per)
        value = (query_buf[b] * conv_buf[b]).astype(bf16)
        for h in range(2):
            out[place(BACK, k, h), :, j * LANES : (j + 1) * LANES] = value


def hold_body(gated, w1, w2, w3, out):
    out[...] = gated[...]


def settle_body(gated, out):
    count, owned, _ = gated.shape
    for h in range(2):
        rows = [gated[place(BACK, k, h)] for k in range(count // 2)]
        out[pl.ds(h * (count // 2) * owned, count // 2 * owned), :] = jnp.concatenate(rows, axis=0)


def columns_of(w, core, half):
    return [w[:, pl.ds(pl.multiple_of((2 * h + core) * half, half), half)] for h in range(2)]


def own_body(core, own, w0, w1, w2, w3, o0, o1, o2, o3):
    half = own.shape[0] // 2
    for w, o in ((w0, o0), (w1, o1), (w2, o2), (w3, o3)):
        o[...] = dot(jnp.concatenate(columns_of(w, core[0], half), axis=1), own[...])


def other_body(core, other, w0, w1, w2, w3, a0, a1, a2, a3, o0, o1, o2, o3):
    half = other.shape[0] // 2
    for w, a, o in ((w2, a2, o2), (w1, a1, o1), (w3, a3, o3), (w0, a0, o0)):
        term = dot(jnp.concatenate(columns_of(w, 1 - core[0], half), axis=1), other[...])
        o[...] = (a[...] + term).astype(o.dtype)


def add_body(o0, o1, o2, o3, out):
    total = o0[...] + o1[...].astype(f32) + o2[...].astype(f32) + o3[...].astype(f32)
    out[...] = total.astype(out.dtype)


def local(features, short_taps, decay, residue, skip_bias, out_weight):
    _, channels, tokens = features.shape
    shards = lax.axis_size("x") * lax.axis_size("zl")
    owned, modes = decay.shape
    blocks = shards * tokens // LANES
    y, zh, core = (lax.axis_index(a) for a in CH)

    columns = short_taps.transpose(0, 2, 1)
    sent = pl.pallas_call(
        pack_body,
        out_shape=pltpu.VMEM((shards, owned, 2 * tokens + LANES), bf16),
        in_specs=[pl.BlockSpec(memory_space=pltpu.HBM)] * 2,
        out_specs=in_vmem,
        scratch_shapes=[
            pltpu.VMEM(features.shape, bf16),
            pltpu.VMEM(columns.shape, f32),
            pltpu.SemaphoreType.DMA((4,)),
        ],
        compiler_params=params(),
        name="pack",
    )(*(pltpu.with_memory_space_constraint(a, pltpu.HBM) for a in (features, columns)))
    held = exchange(sent, GO)

    ys = lax.axis_size("y")
    cols = out_weight.shape[1] // ys
    weights = {0: lax.dynamic_slice_in_dim(out_weight, y * cols, cols, 1)}
    for d in ORDER:
        block = lax.dynamic_slice_in_dim(out_weight, (y + ys - d) % ys * cols, cols, 1)
        weights[d] = shift(block, "y", -d)
    weights = [weights[d] for d in range(ys)]

    mats = pl.pallas_call(
        prep_body,
        out_shape=(
            pltpu.VMEM((2, owned, LANES, LANES), bf16),
            pltpu.VMEM((2, owned * LANES, LANES), bf16),
            pltpu.VMEM((2, LANES, owned * LANES), bf16),
            pltpu.VMEM((8, LANES), f32),
            pltpu.VMEM((3 * TAPS, owned, LANES), f32),
        ),
        in_specs=[in_vmem] * 4,
        out_specs=(in_vmem,) * 5,
        cost_estimate=pl.CostEstimate(flops=2000000, bytes_accessed=1600000, transcendentals=70000),
        compiler_params=params(),
        name="prep",
    )(decay, residue, skip_bias.reshape(1, -1), columns)
    toeplitz, enter, leave, powers, taps = mats
    gated = pl.pallas_call(
        conv_body,
        out_shape=pltpu.VMEM((2 * shards, owned, tokens), bf16),
        in_specs=[in_vmem] * 6,
        out_specs=in_vmem,
        scratch_shapes=[pltpu.VMEM((blocks, owned, LANES), f32)] * 3,
        cost_estimate=pl.CostEstimate(flops=WAIT, bytes_accessed=2500000, transcendentals=0),
        compiler_params=params(),
        name="conv",
    )(*map(near, (held, taps, toeplitz, enter, leave, powers)))
    gated = pl.pallas_call(
        hold_body,
        out_shape=pltpu.VMEM((2 * shards, owned, tokens), bf16),
        in_specs=[in_vmem] + [pl.BlockSpec(memory_space=pl.ANY)] * 3,
        out_specs=in_vmem,
        compiler_params=params(),
        name="hold",
    )(near(gated), *(weights[d] for d in ORDER))
    gated = exchange(gated, BACK)
    gated = pl.pallas_call(
        settle_body,
        out_shape=pltpu.VMEM((2 * channels, tokens), bf16),
        in_specs=[in_vmem],
        out_specs=in_vmem,
        compiler_params=params(),
        name="settle",
    )(near(gated))
    other = shift(gated, "c", 1)
    rows = out_weight.shape[0]
    one = core.reshape(1)
    close = [near(w) for w in weights]
    sums = pl.pallas_call(
        own_body,
        out_shape=(pltpu.VMEM((rows, tokens), f32),) * 4,
        in_specs=[pl.BlockSpec(memory_space=pltpu.SMEM)] + [in_vmem] * 5,
        out_specs=(in_vmem,) * 4,
        cost_estimate=pl.CostEstimate(flops=150000000, bytes_accessed=1500000, transcendentals=0),
        compiler_params=params(),
        name="own",
    )(one, near(gated), *close)
    parts = pl.pallas_call(
        other_body,
        out_shape=(pltpu.VMEM((rows, tokens), f32),) + (pltpu.VMEM((rows, tokens), bf16),) * 3,
        in_specs=[pl.BlockSpec(memory_space=pltpu.SMEM)] + [in_vmem] * 9,
        out_specs=(in_vmem,) * 4,
        cost_estimate=pl.CostEstimate(flops=150000000, bytes_accessed=1500000, transcendentals=0),
        compiler_params=params(),
        name="other",
    )(one, near(other), *close, *map(near, sums))
    arrived = [parts[0]] + [shift(parts[d], "y", d) for d in (1, 2, 3)]
    return pl.pallas_call(
        add_body,
        out_shape=jax.ShapeDtypeStruct((rows, tokens), bf16),
        in_specs=[in_vmem] * 4,
        out_specs=in_vmem,
        compiler_params=params(),
        name="add",
    )(*map(near, arrived))


def solution(mesh):
    split = Mesh(mesh.devices.reshape(4, 4, 4, 2, 2), CTX + CH)
    in_specs = (
        P(None, CH, CTX),
        P(None, CH, None),
        P(CH + CTX, None),
        P(CH + CTX, None),
        P(CH),
        P(CH, None),
    )
    return jax.shard_map(local, mesh=split, in_specs=in_specs, out_specs=P(CH, CTX), check_vma=False)
```

```python
import jax
import jax.numpy as jnp
from jax import lax
from jax.experimental import pallas as pl
from jax.experimental.pallas import tpu as pltpu
from jax.sharding import Mesh
from jax.sharding import PartitionSpec as P

CTX = ("x", "zl")
CH = ("y", "zh", "c")
GO = ("zl", "x")
BACK = ("zl", "x", "zh")
LANES = 128
TAPS = 3
TURN = {16: 4, 32: 0}
ORDER = (2, 1, 3)
WAIT = 20_000_000_000
f32 = jnp.float32
bf16 = jnp.bfloat16
in_vmem = pl.BlockSpec(memory_space=pltpu.VMEM)


def shift(value, axis, steps):
    count = lax.axis_size(axis)
    return lax.ppermute(value, axis, [(i, (i + steps) % count) for i in range(count)])


def place(order, k, h=0):
    at = {"x": k // 4, "zl": k % 4, "zh": h}
    size = {"x": 4, "zl": 4, "zh": 2}
    index, count = 0, 1
    for axis in order:
        index = index * size[axis] + at[axis]
        count *= size[axis]
    return count - 1 - index


def spot(order, k, h=0):
    count = 4 ** 2 * (2 if "zh" in order else 1)
    return lax.rem(place(order, k, h) + lax.axis_index("c") * (count - TURN[count]), count)


def exchange(value, order):
    count = value.shape[0]
    groups = [
        [2 * (count - 1 - (i + c * TURN[count]) % count) + c for i in range(count)] for c in (0, 1)
    ]
    return lax.all_to_all(value, order + ("c",), 0, 0, axis_index_groups=groups, tiled=True)


def near(value):
    return pltpu.with_memory_space_constraint(value, pltpu.VMEM)


def params(**kwargs):
    return pltpu.CompilerParams(vmem_limit_bytes=16 << 20, **kwargs)


def ctx_index():
    return lax.axis_index("x") * lax.axis_size("zl") + lax.axis_index("zl")


def split_store(ref, index, value):
    high = value.astype(bf16)
    ref[(0,) + index] = high
    ref[(1,) + index] = (value - high.astype(f32)).astype(bf16)


def pack_body(features_hbm, taps_hbm, sent, features, short_taps, sem):
    copies = [pltpu.make_async_copy(taps_hbm, short_taps, sem.at[3])]
    for s in range(3):
        copies.append(pltpu.make_async_copy(features_hbm.at[s], features.at[s], sem.at[s]))
    for copy in copies:
        copy.start()
    for copy in copies:
        copy.wait()
    _, channels, tokens = features.shape
    shards, owned, _ = sent.shape
    per = tokens // LANES
    rows = [short_taps[s] for s in range(3)]
    filler = jnp.zeros((LANES - 3 * TAPS, channels), f32)
    columns = jnp.transpose(jnp.concatenate(rows + [filler], axis=0))
    lane = lax.broadcasted_iota(jnp.int32, (owned, LANES), 1)
    zero = jnp.zeros((owned, LANES), f32)
    for k in range(shards):
        at = slice(k * owned, (k + 1) * owned)
        rims = zero
        value = [[], [], []]
        for s in range(3):
            w = [
                jnp.broadcast_to(columns[at, i : i + 1], (owned, LANES))
                for i in range(s * TAPS, (s + 1) * TAPS)
            ]
            last = (zero, zero)
            for j in range(per):
                now = features[s, at, j * LANES : (j + 1) * LANES].astype(f32)
                one, two = pltpu.roll(now, 1, 1), pltpu.roll(now, 2, 1)
                value[s].append(
                    w[0] * now
                    + w[1] * jnp.where(lane < 1, last[0], one)
                    + w[2] * jnp.where(lane < 2, last[1], two)
                )
                last = (one, two)
                if j == 0:
                    head = pltpu.roll(now, 4 * s, 1) if s else now
                    rims = jnp.where((lane == 4 * s) | (lane == 4 * s + 1), head, rims)
                if j == per - 1:
                    tail = pltpu.roll(now, 4 * s + 4, 1)
                    rims = jnp.where((lane == 4 * s + 2) | (lane == 4 * s + 3), tail, rims)
        for j in range(per):
            part = slice(j * LANES, (j + 1) * LANES)
            sent[spot(GO, k), :, part] = (value[1][j] * value[2][j]).astype(bf16)
            part = slice(tokens + j * LANES, tokens + (j + 1) * LANES)
            sent[spot(GO, k), :, part] = value[0][j].astype(bf16)
        sent[spot(GO, k), :, 2 * tokens :] = rims.astype(bf16)


def prep_body(decay, residue, skip_bias, short_taps, toeplitz, enter, leave, powers, taps):
    owned, modes = decay.shape
    lane = lax.broadcasted_iota(jnp.int32, (owned, LANES), 1)
    sub = lax.broadcasted_iota(jnp.int32, (owned, LANES), 0)
    mine = lane == sub + ctx_index() * owned

    def own_column(values):
        picked = jnp.sum(jnp.where(mine, values, 0.0), axis=1, keepdims=True)
        return jnp.broadcast_to(picked, (owned, LANES))

    def as_row(values):
        tiled = jnp.concatenate([values] * owned, axis=1)
        return jnp.sum(jnp.where(lane // modes == sub, tiled, 0.0), axis=0, keepdims=True)

    for s in range(3):
        for j in range(TAPS):
            taps[s * TAPS + j] = own_column(short_taps[s, j : j + 1, :])
    moment = lane.astype(f32)
    impulse = jnp.where(lane == 0, own_column(skip_bias[...]), 0.0)
    rates, weights = decay[...], residue[...]
    for n in range(modes):
        impulse = impulse + weights[:, n : n + 1] * jnp.exp(-rates[:, n : n + 1] * moment)
    row = lax.broadcasted_iota(jnp.int32, (LANES, LANES), 0)
    col = lax.broadcasted_iota(jnp.int32, (LANES, LANES), 1)
    rate = as_row(rates)
    into = jnp.exp(-rate * (LANES - 1 - row).astype(f32))
    out_of = jnp.transpose(as_row(weights) * jnp.exp(-rate * (row + 1).astype(f32)))
    for c in range(owned):
        spread = jnp.broadcast_to(impulse[c : c + 1, :], (LANES, LANES))
        rolled = pltpu.roll(spread, 0, 1, stride=1, stride_axis=0)
        split_store(toeplitz, (c,), jnp.where(col >= row, rolled, 0.0))
        part = pl.ds(c * LANES, LANES)
        split_store(enter, (part, slice(None)), jnp.where(col // modes == c, into, 0.0))
        split_store(leave, (slice(None), part), jnp.where(row // modes == c, out_of, 0.0))
    for i in range(8):
        powers[i : i + 1, :] = jnp.exp(-rate * float(LANES << i))


def dot(a, b):
    return jnp.dot(a, b, preferred_element_type=f32)


def conv_body(held, taps, toeplitz, enter, leave, powers, out, mixed_buf, query_buf, conv_buf):
    shards, owned, _ = held.shape
    tokens = out.shape[-1]
    per = tokens // LANES
    blocks = shards * per
    lane = lax.broadcasted_iota(jnp.int32, (owned, LANES), 1)
    weights = [
        jnp.where(lane < 4, taps[j], jnp.where(lane < 8, taps[TAPS + j], taps[2 * TAPS + j]))
        for j in range(TAPS)
    ]
    before = jnp.zeros((owned, LANES), f32)
    for k in range(shards):
        rims = held[spot(GO, k), :, 2 * tokens :].astype(f32)
        older = pltpu.roll(before, LANES - 2, 1)
        middle = jnp.where(lane % 4 == 0, pltpu.roll(before, LANES - 3, 1), pltpu.roll(rims, 1, 1))
        head = weights[0] * rims + weights[1] * middle + weights[2] * older
        before = rims
        fixed = pltpu.roll(head, LANES - 4, 1) * pltpu.roll(head, LANES - 8, 1)
        for j in range(per):
            now = held[spot(GO, k), :, j * LANES : (j + 1) * LANES].astype(f32)
            query = held[spot(GO, k), :, tokens + j * LANES : tokens + (j + 1) * LANES].astype(f32)
            if j == 0:
                now = jnp.where(lane < 2, fixed.astype(bf16).astype(f32), now)
                query = jnp.where(lane < 2, head, query)
            mixed_buf[k * per + j] = now
            query_buf[k * per + j] = query
    mixed = [mixed_buf[:, c, :].astype(bf16) for c in range(owned)]
    whole = jnp.concatenate(mixed, axis=1)
    state = dot(whole, enter[0]) + dot(whole, enter[1])
    row = lax.broadcasted_iota(jnp.int32, (blocks, LANES), 0)
    step, i = 1, 0
    while step < blocks:
        moved = jnp.where(row < step, 0.0, pltpu.roll(state, step, 0))
        state = state + powers[i : i + 1, :] * moved
        step, i = step * 2, i + 1
    state = jnp.where(row < 1, 0.0, pltpu.roll(state, 1, 0))
    high = state.astype(bf16)
    low = (state - high.astype(f32)).astype(bf16)
    for c in range(owned):
        part = pl.ds(c * LANES, LANES)
        value = dot(mixed[c], toeplitz[0, c]) + dot(mixed[c], toeplitz[1, c])
        value = value + dot(high, leave[0, :, part]) + dot(high, leave[1, :, part])
        conv_buf[:, c, :] = value + dot(low, leave[0, :, part])
    for b in range(blocks):
        k, j = divmod(b, per)
        value = (query_buf[b] * conv_buf[b]).astype(bf16)
        for h in range(2):
            out[spot(BACK, k, h), :, j * LANES : (j + 1) * LANES] = value


def hold_body(gated, w1, w2, w3, out):
    out[...] = gated[...]


def settle_body(gated, out):
    count, owned, _ = gated.shape
    for h in range(2):
        rows = [gated[spot(BACK, k, h)] for k in range(count // 2)]
        out[pl.ds(h * (count // 2) * owned, count // 2 * owned), :] = jnp.concatenate(rows, axis=0)


def columns_of(w, core, half):
    return [w[:, pl.ds(pl.multiple_of((2 * h + core) * half, half), half)] for h in range(2)]


def own_body(core, own, w0, w1, w2, w3, o0, o1, o2, o3):
    half = own.shape[0] // 2
    for w, o in ((w0, o0), (w1, o1), (w2, o2), (w3, o3)):
        o[...] = dot(jnp.concatenate(columns_of(w, core[0], half), axis=1), own[...])


def other_body(core, other, w0, w1, w2, w3, a0, a1, a2, a3, o0, o1, o2, o3):
    half = other.shape[0] // 2
    for w, a, o in ((w2, a2, o2), (w1, a1, o1), (w3, a3, o3), (w0, a0, o0)):
        term = dot(jnp.concatenate(columns_of(w, 1 - core[0], half), axis=1), other[...])
        o[...] = (a[...] + term).astype(o.dtype)


def add_body(o0, o1, o2, o3, out):
    total = o0[...] + o1[...].astype(f32) + o2[...].astype(f32) + o3[...].astype(f32)
    out[...] = total.astype(out.dtype)


def local(features, short_taps, decay, residue, skip_bias, out_weight):
    _, channels, tokens = features.shape
    shards = lax.axis_size("x") * lax.axis_size("zl")
    owned, modes = decay.shape
    blocks = shards * tokens // LANES
    y, zh, core = (lax.axis_index(a) for a in CH)

    columns = short_taps.transpose(0, 2, 1)
    sent = pl.pallas_call(
        pack_body,
        out_shape=pltpu.VMEM((shards, owned, 2 * tokens + LANES), bf16),
        in_specs=[pl.BlockSpec(memory_space=pltpu.HBM)] * 2,
        out_specs=in_vmem,
        scratch_shapes=[
            pltpu.VMEM(features.shape, bf16),
            pltpu.VMEM(columns.shape, f32),
            pltpu.SemaphoreType.DMA((4,)),
        ],
        compiler_params=params(),
        name="pack",
    )(*(pltpu.with_memory_space_constraint(a, pltpu.HBM) for a in (features, columns)))
    held = exchange(sent, GO)

    ys = lax.axis_size("y")
    cols = out_weight.shape[1] // ys
    weights = {0: lax.dynamic_slice_in_dim(out_weight, y * cols, cols, 1)}
    for d in ORDER:
        block = lax.dynamic_slice_in_dim(out_weight, (y + ys - d) % ys * cols, cols, 1)
        weights[d] = shift(block, "y", -d)
    weights = [weights[d] for d in range(ys)]

    mats = pl.pallas_call(
        prep_body,
        out_shape=(
            pltpu.VMEM((2, owned, LANES, LANES), bf16),
            pltpu.VMEM((2, owned * LANES, LANES), bf16),
            pltpu.VMEM((2, LANES, owned * LANES), bf16),
            pltpu.VMEM((8, LANES), f32),
            pltpu.VMEM((3 * TAPS, owned, LANES), f32),
        ),
        in_specs=[in_vmem] * 4,
        out_specs=(in_vmem,) * 5,
        cost_estimate=pl.CostEstimate(flops=2000000, bytes_accessed=1600000, transcendentals=70000),
        compiler_params=params(),
        name="prep",
    )(decay, residue, skip_bias.reshape(1, -1), columns)
    toeplitz, enter, leave, powers, taps = mats
    gated = pl.pallas_call(
        conv_body,
        out_shape=pltpu.VMEM((2 * shards, owned, tokens), bf16),
        in_specs=[in_vmem] * 6,
        out_specs=in_vmem,
        scratch_shapes=[pltpu.VMEM((blocks, owned, LANES), f32)] * 3,
        cost_estimate=pl.CostEstimate(flops=WAIT, bytes_accessed=2500000, transcendentals=0),
        compiler_params=params(),
        name="conv",
    )(*map(near, (held, taps, toeplitz, enter, leave, powers)))
    gated = pl.pallas_call(
        hold_body,
        out_shape=pltpu.VMEM((2 * shards, owned, tokens), bf16),
        in_specs=[in_vmem] + [pl.BlockSpec(memory_space=pl.ANY)] * 3,
        out_specs=in_vmem,
        compiler_params=params(),
        name="hold",
    )(near(gated), *(weights[d] for d in ORDER))
    gated = exchange(gated, BACK)
    gated = pl.pallas_call(
        settle_body,
        out_shape=pltpu.VMEM((2 * channels, tokens), bf16),
        in_specs=[in_vmem],
        out_specs=in_vmem,
        compiler_params=params(),
        name="settle",
    )(near(gated))
    other = shift(gated, "c", 1)
    rows = out_weight.shape[0]
    one = core.reshape(1)
    close = [near(w) for w in weights]
    sums = pl.pallas_call(
        own_body,
        out_shape=(pltpu.VMEM((rows, tokens), f32),) * 4,
        in_specs=[pl.BlockSpec(memory_space=pltpu.SMEM)] + [in_vmem] * 5,
        out_specs=(in_vmem,) * 4,
        cost_estimate=pl.CostEstimate(flops=150000000, bytes_accessed=1500000, transcendentals=0),
        compiler_params=params(),
        name="own",
    )(one, near(gated), *close)
    parts = pl.pallas_call(
        other_body,
        out_shape=(pltpu.VMEM((rows, tokens), f32),) + (pltpu.VMEM((rows, tokens), bf16),) * 3,
        in_specs=[pl.BlockSpec(memory_space=pltpu.SMEM)] + [in_vmem] * 9,
        out_specs=(in_vmem,) * 4,
        cost_estimate=pl.CostEstimate(flops=150000000, bytes_accessed=1500000, transcendentals=0),
        compiler_params=params(),
        name="other",
    )(one, near(other), *close, *map(near, sums))
    arrived = [parts[0]] + [shift(parts[d], "y", d) for d in (2, 1, 3)]
    return pl.pallas_call(
        add_body,
        out_shape=jax.ShapeDtypeStruct((rows, tokens), bf16),
        in_specs=[in_vmem] * 4,
        out_specs=in_vmem,
        compiler_params=params(),
        name="add",
    )(*map(near, arrived))


def solution(mesh):
    split = Mesh(mesh.devices.reshape(4, 4, 4, 2, 2), CTX + CH)
    in_specs = (
        P(None, CH, CTX),
        P(None, CH, None),
        P(CH + CTX, None),
        P(CH + CTX, None),
        P(CH),
        P(CH, None),
    )
    return jax.shard_map(local, mesh=split, in_specs=in_specs, out_specs=P(CH, CTX), check_vma=False)
```

```python
import jax
import jax.numpy as jnp
from jax import lax
from jax.experimental import pallas as pl
from jax.experimental.pallas import tpu as pltpu
from jax.sharding import Mesh
from jax.sharding import PartitionSpec as P

CTX = ("x", "zl")
CH = ("y", "zh", "c")
GO = ("zl", "x")
BACK = ("zl", "x", "zh")
LANES = 128
TAPS = 3
TURN = {16: (8, 4), 32: (4, 0)}
ORDER = (2, 1, 3)
WAIT = 20_000_000_000
f32 = jnp.float32
bf16 = jnp.bfloat16
in_vmem = pl.BlockSpec(memory_space=pltpu.VMEM)


def shift(value, axis, steps):
    count = lax.axis_size(axis)
    return lax.ppermute(value, axis, [(i, (i + steps) % count) for i in range(count)])


def place(order, k, h=0):
    at = {"x": k // 4, "zl": k % 4, "zh": h}
    size = {"x": 4, "zl": 4, "zh": 2}
    index, count = 0, 1
    for axis in order:
        index = index * size[axis] + at[axis]
        count *= size[axis]
    return count - 1 - index


def spot(order, k, h=0):
    count = 4 ** 2 * (2 if "zh" in order else 1)
    first, second = TURN[count]
    turned = jnp.where(lax.axis_index("c") == 0, count - first, count - second)
    return lax.rem(place(order, k, h) + turned, count)


def exchange(value, order):
    count = value.shape[0]
    groups = [
        [2 * (count - 1 - (i + TURN[count][c]) % count) + c for i in range(count)] for c in (0, 1)
    ]
    return lax.all_to_all(value, order + ("c",), 0, 0, axis_index_groups=groups, tiled=True)


def near(value):
    return pltpu.with_memory_space_constraint(value, pltpu.VMEM)


def params(**kwargs):
    return pltpu.CompilerParams(vmem_limit_bytes=16 << 20, **kwargs)


def ctx_index():
    return lax.axis_index("x") * lax.axis_size("zl") + lax.axis_index("zl")


def split(value):
    high = value.astype(bf16)
    return high, (value - high.astype(f32)).astype(bf16)


def pack_body(features_hbm, taps_hbm, sent, features, short_taps, sem):
    copies = [pltpu.make_async_copy(taps_hbm, short_taps, sem.at[3])]
    for s in range(3):
        copies.append(pltpu.make_async_copy(features_hbm.at[s], features.at[s], sem.at[s]))
    for copy in copies:
        copy.start()
    for copy in copies:
        copy.wait()
    _, channels, tokens = features.shape
    shards, owned, _ = sent.shape
    per = tokens // LANES
    rows = [short_taps[s] for s in range(3)]
    filler = jnp.zeros((LANES - 3 * TAPS, channels), f32)
    columns = jnp.transpose(jnp.concatenate(rows + [filler], axis=0))
    lane = lax.broadcasted_iota(jnp.int32, (owned, LANES), 1)
    zero = jnp.zeros((owned, LANES), f32)
    for k in range(shards):
        at = slice(k * owned, (k + 1) * owned)
        rims = zero
        value = [[], [], []]
        for s in range(3):
            w = [
                jnp.broadcast_to(columns[at, i : i + 1], (owned, LANES))
                for i in range(s * TAPS, (s + 1) * TAPS)
            ]
            last = (zero, zero)
            for j in range(per):
                now = features[s, at, j * LANES : (j + 1) * LANES].astype(f32)
                one, two = pltpu.roll(now, 1, 1), pltpu.roll(now, 2, 1)
                value[s].append(
                    w[0] * now
                    + w[1] * jnp.where(lane < 1, last[0], one)
                    + w[2] * jnp.where(lane < 2, last[1], two)
                )
                last = (one, two)
                if j == 0:
                    head = pltpu.roll(now, 4 * s, 1) if s else now
                    rims = jnp.where((lane == 4 * s) | (lane == 4 * s + 1), head, rims)
                if j == per - 1:
                    tail = pltpu.roll(now, 4 * s + 4, 1)
                    rims = jnp.where((lane == 4 * s + 2) | (lane == 4 * s + 3), tail, rims)
        for j in range(per):
            part = slice(j * LANES, (j + 1) * LANES)
            sent[spot(GO, k), :, part] = (value[1][j] * value[2][j]).astype(bf16)
            part = slice(tokens + j * LANES, tokens + (j + 1) * LANES)
            sent[spot(GO, k), :, part] = value[0][j].astype(bf16)
        sent[spot(GO, k), :, 2 * tokens :] = rims.astype(bf16)


def prep_body(decay, residue, skip_bias, short_taps, toeplitz, enter, leave, powers, taps):
    owned, modes = decay.shape
    lane = lax.broadcasted_iota(jnp.int32, (owned, LANES), 1)
    sub = lax.broadcasted_iota(jnp.int32, (owned, LANES), 0)
    mine = lane == sub + ctx_index() * owned

    def own_column(values):
        picked = jnp.sum(jnp.where(mine, values, 0.0), axis=1, keepdims=True)
        return jnp.broadcast_to(picked, (owned, LANES))

    def as_row(values):
        tiled = jnp.concatenate([values] * owned, axis=1)
        return jnp.sum(jnp.where(lane // modes == sub, tiled, 0.0), axis=0, keepdims=True)

    for s in range(3):
        for j in range(TAPS):
            taps[s * TAPS + j] = own_column(short_taps[s, j : j + 1, :])
    moment = lane.astype(f32)
    impulse = jnp.where(lane == 0, own_column(skip_bias[...]), 0.0)
    rates, weights = decay[...], residue[...]
    for n in range(modes):
        impulse = impulse + weights[:, n : n + 1] * jnp.exp(-rates[:, n : n + 1] * moment)
    row = lax.broadcasted_iota(jnp.int32, (LANES, LANES), 0)
    col = lax.broadcasted_iota(jnp.int32, (LANES, LANES), 1)
    rate = as_row(rates)
    into = jnp.exp(-rate * (LANES - 1 - row).astype(f32))
    out_of = jnp.transpose(as_row(weights) * jnp.exp(-rate * (row + 1).astype(f32)))
    for c in range(owned):
        spread = jnp.broadcast_to(impulse[c : c + 1, :], (LANES, LANES))
        rolled = pltpu.roll(spread, 0, 1, stride=1, stride_axis=0)
        high, low = split(jnp.where(col >= row, rolled, 0.0))
        toeplitz[c, :LANES, :] = high
        toeplitz[c, LANES:, :] = low
        part = slice(c * LANES, (c + 1) * LANES)
        high, low = split(jnp.where(col // modes == c, into, 0.0))
        enter[part, :LANES] = high
        enter[part, LANES:] = low
        high, low = split(jnp.where(row // modes == c, out_of, 0.0))
        leave[:LANES, part] = high
        leave[LANES : 2 * LANES, part] = high
        leave[2 * LANES :, part] = low
    for i in range(8):
        powers[i : i + 1, :] = jnp.exp(-rate * float(LANES << i))


def dot(a, b):
    return jnp.dot(a, b, preferred_element_type=f32)


def conv_body(held, taps, toeplitz, enter, leave, powers, out, mixed_buf, query_buf, conv_buf):
    shards, owned, _ = held.shape
    tokens = out.shape[-1]
    per = tokens // LANES
    blocks = shards * per
    lane = lax.broadcasted_iota(jnp.int32, (owned, LANES), 1)
    weights = [
        jnp.where(lane < 4, taps[j], jnp.where(lane < 8, taps[TAPS + j], taps[2 * TAPS + j]))
        for j in range(TAPS)
    ]
    before = jnp.zeros((owned, LANES), f32)
    for k in range(shards):
        rims = held[spot(GO, k), :, 2 * tokens :].astype(f32)
        older = pltpu.roll(before, LANES - 2, 1)
        middle = jnp.where(lane % 4 == 0, pltpu.roll(before, LANES - 3, 1), pltpu.roll(rims, 1, 1))
        head = weights[0] * rims + weights[1] * middle + weights[2] * older
        before = rims
        fixed = pltpu.roll(head, LANES - 4, 1) * pltpu.roll(head, LANES - 8, 1)
        for j in range(per):
            now = held[spot(GO, k), :, j * LANES : (j + 1) * LANES].astype(f32)
            query = held[spot(GO, k), :, tokens + j * LANES : tokens + (j + 1) * LANES].astype(f32)
            if j == 0:
                now = jnp.where(lane < 2, fixed.astype(bf16).astype(f32), now)
                query = jnp.where(lane < 2, head, query)
            mixed_buf[k * per + j] = now
            query_buf[k * per + j] = query
    mixed = [mixed_buf[:, c, :].astype(bf16) for c in range(owned)]
    whole = jnp.concatenate(mixed, axis=1)
    state = dot(whole, enter[...])
    state = state[:, :LANES] + state[:, LANES:]
    row = lax.broadcasted_iota(jnp.int32, (blocks, LANES), 0)
    step, i = 1, 0
    while step < blocks:
        moved = jnp.where(row < step, 0.0, pltpu.roll(state, step, 0))
        state = state + powers[i : i + 1, :] * moved
        step, i = step * 2, i + 1
    state = jnp.where(row < 1, 0.0, pltpu.roll(state, 1, 0))
    high, low = split(state)
    carried = dot(jnp.concatenate([high, low, high], axis=1), leave[...])
    for c in range(owned):
        value = dot(jnp.concatenate([mixed[c], mixed[c]], axis=1), toeplitz[c])
        conv_buf[:, c, :] = value + carried[:, c * LANES : (c + 1) * LANES]
    for b in range(blocks):
        k, j = divmod(b, per)
        value = (query_buf[b] * conv_buf[b]).astype(bf16)
        for h in range(2):
            out[spot(BACK, k, h), :, j * LANES : (j + 1) * LANES] = value


def hold_body(gated, w1, w2, w3, out):
    out[...] = gated[...]


def settle_body(gated, out):
    count, owned, _ = gated.shape
    for h in range(2):
        rows = [gated[spot(BACK, k, h)] for k in range(count // 2)]
        out[pl.ds(h * (count // 2) * owned, count // 2 * owned), :] = jnp.concatenate(rows, axis=0)


def columns_of(w, core, half):
    return [w[:, pl.ds(pl.multiple_of((2 * h + core) * half, half), half)] for h in range(2)]


def own_body(core, own, w0, w1, w2, w3, o0, o1, o2, o3):
    half = own.shape[0] // 2
    for w, o in ((w0, o0), (w1, o1), (w2, o2), (w3, o3)):
        o[...] = dot(jnp.concatenate(columns_of(w, core[0], half), axis=1), own[...])


def other_body(core, other, w0, w1, w2, w3, a0, a1, a2, a3, o0, o1, o2, o3):
    half = other.shape[0] // 2
    for w, a, o in ((w2, a2, o2), (w1, a1, o1), (w3, a3, o3), (w0, a0, o0)):
        term = dot(jnp.concatenate(columns_of(w, 1 - core[0], half), axis=1), other[...])
        o[...] = (a[...] + term).astype(o.dtype)


def add_body(o0, o1, o2, o3, out):
    total = o0[...] + o1[...].astype(f32) + o2[...].astype(f32) + o3[...].astype(f32)
    out[...] = total.astype(out.dtype)


def local(features, short_taps, decay, residue, skip_bias, out_weight):
    _, channels, tokens = features.shape
    shards = lax.axis_size("x") * lax.axis_size("zl")
    owned, modes = decay.shape
    blocks = shards * tokens // LANES
    y, zh, core = (lax.axis_index(a) for a in CH)

    columns = short_taps.transpose(0, 2, 1)
    sent = pl.pallas_call(
        pack_body,
        out_shape=pltpu.VMEM((shards, owned, 2 * tokens + LANES), bf16),
        in_specs=[pl.BlockSpec(memory_space=pltpu.HBM)] * 2,
        out_specs=in_vmem,
        scratch_shapes=[
            pltpu.VMEM(features.shape, bf16),
            pltpu.VMEM(columns.shape, f32),
            pltpu.SemaphoreType.DMA((4,)),
        ],
        compiler_params=params(),
        name="pack",
    )(*(pltpu.with_memory_space_constraint(a, pltpu.HBM) for a in (features, columns)))
    held = exchange(sent, GO)

    ys = lax.axis_size("y")
    cols = out_weight.shape[1] // ys
    weights = {0: lax.dynamic_slice_in_dim(out_weight, y * cols, cols, 1)}
    for d in ORDER:
        block = lax.dynamic_slice_in_dim(out_weight, (y + ys - d) % ys * cols, cols, 1)
        weights[d] = shift(block, "y", -d)
    weights = [weights[d] for d in range(ys)]

    mats = pl.pallas_call(
        prep_body,
        out_shape=(
            pltpu.VMEM((owned, 2 * LANES, LANES), bf16),
            pltpu.VMEM((owned * LANES, 2 * LANES), bf16),
            pltpu.VMEM((3 * LANES, owned * LANES), bf16),
            pltpu.VMEM((8, LANES), f32),
            pltpu.VMEM((3 * TAPS, owned, LANES), f32),
        ),
        in_specs=[in_vmem] * 4,
        out_specs=(in_vmem,) * 5,
        cost_estimate=pl.CostEstimate(flops=2000000, bytes_accessed=1600000, transcendentals=70000),
        compiler_params=params(),
        name="prep",
    )(decay, residue, skip_bias.reshape(1, -1), columns)
    toeplitz, enter, leave, powers, taps = mats
    gated = pl.pallas_call(
        conv_body,
        out_shape=pltpu.VMEM((2 * shards, owned, tokens), bf16),
        in_specs=[in_vmem] * 6,
        out_specs=in_vmem,
        scratch_shapes=[pltpu.VMEM((blocks, owned, LANES), f32)] * 3,
        cost_estimate=pl.CostEstimate(flops=WAIT, bytes_accessed=2500000, transcendentals=0),
        compiler_params=params(),
        name="conv",
    )(*map(near, (held, taps, toeplitz, enter, leave, powers)))
    gated = pl.pallas_call(
        hold_body,
        out_shape=pltpu.VMEM((2 * shards, owned, tokens), bf16),
        in_specs=[in_vmem] + [pl.BlockSpec(memory_space=pl.ANY)] * 3,
        out_specs=in_vmem,
        compiler_params=params(),
        name="hold",
    )(near(gated), *(weights[d] for d in ORDER))
    gated = exchange(gated, BACK)
    gated = pl.pallas_call(
        settle_body,
        out_shape=pltpu.VMEM((2 * channels, tokens), bf16),
        in_specs=[in_vmem],
        out_specs=in_vmem,
        compiler_params=params(),
        name="settle",
    )(near(gated))
    other = shift(gated, "c", 1)
    rows = out_weight.shape[0]
    one = core.reshape(1)
    close = [near(w) for w in weights]
    sums = pl.pallas_call(
        own_body,
        out_shape=(pltpu.VMEM((rows, tokens), f32),) * 4,
        in_specs=[pl.BlockSpec(memory_space=pltpu.SMEM)] + [in_vmem] * 5,
        out_specs=(in_vmem,) * 4,
        cost_estimate=pl.CostEstimate(flops=150000000, bytes_accessed=1500000, transcendentals=0),
        compiler_params=params(),
        name="own",
    )(one, near(gated), *close)
    parts = pl.pallas_call(
        other_body,
        out_shape=(pltpu.VMEM((rows, tokens), f32),) + (pltpu.VMEM((rows, tokens), bf16),) * 3,
        in_specs=[pl.BlockSpec(memory_space=pltpu.SMEM)] + [in_vmem] * 9,
        out_specs=(in_vmem,) * 4,
        cost_estimate=pl.CostEstimate(flops=150000000, bytes_accessed=1500000, transcendentals=0),
        compiler_params=params(),
        name="other",
    )(one, near(other), *close, *map(near, sums))
    arrived = [parts[0]] + [shift(parts[d], "y", d) for d in (2, 1, 3)]
    return pl.pallas_call(
        add_body,
        out_shape=jax.ShapeDtypeStruct((rows, tokens), bf16),
        in_specs=[in_vmem] * 4,
        out_specs=in_vmem,
        compiler_params=params(),
        name="add",
    )(*map(near, arrived))


def solution(mesh):
    split = Mesh(mesh.devices.reshape(4, 4, 4, 2, 2), CTX + CH)
    in_specs = (
        P(None, CH, CTX),
        P(None, CH, None),
        P(CH + CTX, None),
        P(CH + CTX, None),
        P(CH),
        P(CH, None),
    )
    return jax.shard_map(local, mesh=split, in_specs=in_specs, out_specs=P(CH, CTX), check_vma=False)
```

```python
import jax
import jax.numpy as jnp
from jax import lax
from jax.experimental import pallas as pl
from jax.experimental.pallas import tpu as pltpu
from jax.sharding import Mesh
from jax.sharding import PartitionSpec as P

CTX = ("x", "zl")
CH = ("y", "zh", "c")
GO = ("zl", "x")
BACK = ("zl", "x", "zh")
LANES = 128
TAPS = 3
TURN = {16: (8, 4), 32: (20, 4)}
ORDER = (2, 1, 3)
WAIT = 20_000_000_000
f32 = jnp.float32
bf16 = jnp.bfloat16
in_vmem = pl.BlockSpec(memory_space=pltpu.VMEM)


def shift(value, axis, steps):
    count = lax.axis_size(axis)
    return lax.ppermute(value, axis, [(i, (i + steps) % count) for i in range(count)])


def place(order, k, h=0):
    at = {"x": k // 4, "zl": k % 4, "zh": h}
    size = {"x": 4, "zl": 4, "zh": 2}
    index, count = 0, 1
    for axis in order:
        index = index * size[axis] + at[axis]
        count *= size[axis]
    return count - 1 - index


def spot(order, k, h=0):
    count = 4 ** 2 * (2 if "zh" in order else 1)
    first, second = TURN[count]
    turned = jnp.where(lax.axis_index("c") == 0, count - first, count - second)
    return lax.rem(place(order, k, h) + turned, count)


def exchange(value, order):
    count = value.shape[0]
    groups = [
        [2 * (count - 1 - (i + TURN[count][c]) % count) + c for i in range(count)] for c in (0, 1)
    ]
    return lax.all_to_all(value, order + ("c",), 0, 0, axis_index_groups=groups, tiled=True)


def near(value):
    return pltpu.with_memory_space_constraint(value, pltpu.VMEM)


def params(**kwargs):
    return pltpu.CompilerParams(vmem_limit_bytes=16 << 20, **kwargs)


def ctx_index():
    return lax.axis_index("x") * lax.axis_size("zl") + lax.axis_index("zl")


def split(value):
    high = value.astype(bf16)
    return high, (value - high.astype(f32)).astype(bf16)


def pack_body(features_hbm, taps_hbm, sent, features, short_taps, sem):
    copies = [pltpu.make_async_copy(taps_hbm, short_taps, sem.at[3])]
    for s in range(3):
        copies.append(pltpu.make_async_copy(features_hbm.at[s], features.at[s], sem.at[s]))
    for copy in copies:
        copy.start()
    for copy in copies:
        copy.wait()
    _, channels, tokens = features.shape
    shards, owned, _ = sent.shape
    per = tokens // LANES
    rows = [short_taps[s] for s in range(3)]
    filler = jnp.zeros((LANES - 3 * TAPS, channels), f32)
    columns = jnp.transpose(jnp.concatenate(rows + [filler], axis=0))
    lane = lax.broadcasted_iota(jnp.int32, (owned, LANES), 1)
    zero = jnp.zeros((owned, LANES), f32)
    for k in range(shards):
        at = slice(k * owned, (k + 1) * owned)
        rims = zero
        value = [[], [], []]
        for s in range(3):
            w = [
                jnp.broadcast_to(columns[at, i : i + 1], (owned, LANES))
                for i in range(s * TAPS, (s + 1) * TAPS)
            ]
            last = (zero, zero)
            for j in range(per):
                now = features[s, at, j * LANES : (j + 1) * LANES].astype(f32)
                one, two = pltpu.roll(now, 1, 1), pltpu.roll(now, 2, 1)
                value[s].append(
                    w[0] * now
                    + w[1] * jnp.where(lane < 1, last[0], one)
                    + w[2] * jnp.where(lane < 2, last[1], two)
                )
                last = (one, two)
                if j == 0:
                    head = pltpu.roll(now, 4 * s, 1) if s else now
                    rims = jnp.where((lane == 4 * s) | (lane == 4 * s + 1), head, rims)
                if j == per - 1:
                    tail = pltpu.roll(now, 4 * s + 4, 1)
                    rims = jnp.where((lane == 4 * s + 2) | (lane == 4 * s + 3), tail, rims)
        for j in range(per):
            part = slice(j * LANES, (j + 1) * LANES)
            sent[spot(GO, k), :, part] = (value[1][j] * value[2][j]).astype(bf16)
            part = slice(tokens + j * LANES, tokens + (j + 1) * LANES)
            sent[spot(GO, k), :, part] = value[0][j].astype(bf16)
        sent[spot(GO, k), :, 2 * tokens :] = rims.astype(bf16)


def prep_body(decay, residue, skip_bias, short_taps, toeplitz, enter, leave, powers, taps):
    owned, modes = decay.shape
    lane = lax.broadcasted_iota(jnp.int32, (owned, LANES), 1)
    sub = lax.broadcasted_iota(jnp.int32, (owned, LANES), 0)
    mine = lane == sub + ctx_index() * owned

    def own_column(values):
        picked = jnp.sum(jnp.where(mine, values, 0.0), axis=1, keepdims=True)
        return jnp.broadcast_to(picked, (owned, LANES))

    def as_row(values):
        tiled = jnp.concatenate([values] * owned, axis=1)
        return jnp.sum(jnp.where(lane // modes == sub, tiled, 0.0), axis=0, keepdims=True)

    for s in range(3):
        for j in range(TAPS):
            taps[s * TAPS + j] = own_column(short_taps[s, j : j + 1, :])
    moment = lane.astype(f32)
    impulse = jnp.where(lane == 0, own_column(skip_bias[...]), 0.0)
    rates, weights = decay[...], residue[...]
    for n in range(modes):
        impulse = impulse + weights[:, n : n + 1] * jnp.exp(-rates[:, n : n + 1] * moment)
    row = lax.broadcasted_iota(jnp.int32, (LANES, LANES), 0)
    col = lax.broadcasted_iota(jnp.int32, (LANES, LANES), 1)
    rate = as_row(rates)
    into = jnp.exp(-rate * (LANES - 1 - row).astype(f32))
    out_of = jnp.transpose(as_row(weights) * jnp.exp(-rate * (row + 1).astype(f32)))
    for c in range(owned):
        spread = jnp.broadcast_to(impulse[c : c + 1, :], (LANES, LANES))
        rolled = pltpu.roll(spread, 0, 1, stride=1, stride_axis=0)
        high, low = split(jnp.where(col >= row, rolled, 0.0))
        toeplitz[c, :LANES, :] = high
        toeplitz[c, LANES:, :] = low
        part = slice(c * LANES, (c + 1) * LANES)
        high, low = split(jnp.where(col // modes == c, into, 0.0))
        enter[part, :LANES] = high
        enter[part, LANES:] = low
        high, low = split(jnp.where(row // modes == c, out_of, 0.0))
        leave[:LANES, part] = high
        leave[LANES : 2 * LANES, part] = high
        leave[2 * LANES :, part] = low
    for i in range(8):
        powers[i : i + 1, :] = jnp.exp(-rate * float(LANES << i))


def dot(a, b):
    return jnp.dot(a, b, preferred_element_type=f32)


def conv_body(held, taps, toeplitz, enter, leave, powers, out, mixed_buf, query_buf, conv_buf):
    shards, owned, _ = held.shape
    tokens = out.shape[-1]
    per = tokens // LANES
    blocks = shards * per
    lane = lax.broadcasted_iota(jnp.int32, (owned, LANES), 1)
    weights = [
        jnp.where(lane < 4, taps[j], jnp.where(lane < 8, taps[TAPS + j], taps[2 * TAPS + j]))
        for j in range(TAPS)
    ]
    before = jnp.zeros((owned, LANES), f32)
    for k in range(shards):
        rims = held[spot(GO, k), :, 2 * tokens :].astype(f32)
        older = pltpu.roll(before, LANES - 2, 1)
        middle = jnp.where(lane % 4 == 0, pltpu.roll(before, LANES - 3, 1), pltpu.roll(rims, 1, 1))
        head = weights[0] * rims + weights[1] * middle + weights[2] * older
        before = rims
        fixed = pltpu.roll(head, LANES - 4, 1) * pltpu.roll(head, LANES - 8, 1)
        for j in range(per):
            now = held[spot(GO, k), :, j * LANES : (j + 1) * LANES].astype(f32)
            query = held[spot(GO, k), :, tokens + j * LANES : tokens + (j + 1) * LANES].astype(f32)
            if j == 0:
                now = jnp.where(lane < 2, fixed.astype(bf16).astype(f32), now)
                query = jnp.where(lane < 2, head, query)
            mixed_buf[k * per + j] = now
            query_buf[k * per + j] = query
    mixed = [mixed_buf[:, c, :].astype(bf16) for c in range(owned)]
    whole = jnp.concatenate(mixed, axis=1)
    state = dot(whole, enter[...])
    state = state[:, :LANES] + state[:, LANES:]
    row = lax.broadcasted_iota(jnp.int32, (blocks, LANES), 0)
    step, i = 1, 0
    while step < blocks:
        moved = jnp.where(row < step, 0.0, pltpu.roll(state, step, 0))
        state = state + powers[i : i + 1, :] * moved
        step, i = step * 2, i + 1
    state = jnp.where(row < 1, 0.0, pltpu.roll(state, 1, 0))
    high, low = split(state)
    carried = dot(jnp.concatenate([high, low, high], axis=1), leave[...])
    for c in range(owned):
        value = dot(jnp.concatenate([mixed[c], mixed[c]], axis=1), toeplitz[c])
        conv_buf[:, c, :] = value + carried[:, c * LANES : (c + 1) * LANES]
    for b in range(blocks):
        k, j = divmod(b, per)
        value = (query_buf[b] * conv_buf[b]).astype(bf16)
        for h in range(2):
            out[spot(BACK, k, h), :, j * LANES : (j + 1) * LANES] = value


def hold_body(gated, w1, w2, w3, out):
    out[...] = gated[...]


def settle_body(gated, out):
    count, owned, _ = gated.shape
    for h in range(2):
        rows = [gated[spot(BACK, k, h)] for k in range(count // 2)]
        out[pl.ds(h * (count // 2) * owned, count // 2 * owned), :] = jnp.concatenate(rows, axis=0)


def columns_of(w, core, half):
    return [w[:, pl.ds(pl.multiple_of((2 * h + core) * half, half), half)] for h in range(2)]


def own_body(core, own, w0, w1, w2, w3, o0, o1, o2, o3):
    half = own.shape[0] // 2
    for w, o in ((w0, o0), (w1, o1), (w2, o2), (w3, o3)):
        o[...] = dot(jnp.concatenate(columns_of(w, core[0], half), axis=1), own[...])


def other_body(core, other, w0, w1, w2, w3, a0, a1, a2, a3, o0, o1, o2, o3):
    half = other.shape[0] // 2
    for w, a, o in ((w2, a2, o2), (w1, a1, o1), (w3, a3, o3), (w0, a0, o0)):
        term = dot(jnp.concatenate(columns_of(w, 1 - core[0], half), axis=1), other[...])
        o[...] = (a[...] + term).astype(o.dtype)


def add_body(o0, o1, o2, o3, out):
    total = o0[...] + o1[...].astype(f32) + o2[...].astype(f32) + o3[...].astype(f32)
    out[...] = total.astype(out.dtype)


def local(features, short_taps, decay, residue, skip_bias, out_weight):
    _, channels, tokens = features.shape
    shards = lax.axis_size("x") * lax.axis_size("zl")
    owned, modes = decay.shape
    blocks = shards * tokens // LANES
    y, zh, core = (lax.axis_index(a) for a in CH)

    columns = short_taps.transpose(0, 2, 1)
    sent = pl.pallas_call(
        pack_body,
        out_shape=pltpu.VMEM((shards, owned, 2 * tokens + LANES), bf16),
        in_specs=[pl.BlockSpec(memory_space=pltpu.HBM)] * 2,
        out_specs=in_vmem,
        scratch_shapes=[
            pltpu.VMEM(features.shape, bf16),
            pltpu.VMEM(columns.shape, f32),
            pltpu.SemaphoreType.DMA((4,)),
        ],
        compiler_params=params(),
        name="pack",
    )(*(pltpu.with_memory_space_constraint(a, pltpu.HBM) for a in (features, columns)))
    held = exchange(sent, GO)

    ys = lax.axis_size("y")
    cols = out_weight.shape[1] // ys
    weights = {0: lax.dynamic_slice_in_dim(out_weight, y * cols, cols, 1)}
    for d in ORDER:
        block = lax.dynamic_slice_in_dim(out_weight, (y + ys - d) % ys * cols, cols, 1)
        weights[d] = shift(block, "y", -d)
    weights = [weights[d] for d in range(ys)]

    mats = pl.pallas_call(
        prep_body,
        out_shape=(
            pltpu.VMEM((owned, 2 * LANES, LANES), bf16),
            pltpu.VMEM((owned * LANES, 2 * LANES), bf16),
            pltpu.VMEM((3 * LANES, owned * LANES), bf16),
            pltpu.VMEM((8, LANES), f32),
            pltpu.VMEM((3 * TAPS, owned, LANES), f32),
        ),
        in_specs=[in_vmem] * 4,
        out_specs=(in_vmem,) * 5,
        cost_estimate=pl.CostEstimate(flops=2000000, bytes_accessed=1600000, transcendentals=70000),
        compiler_params=params(),
        name="prep",
    )(decay, residue, skip_bias.reshape(1, -1), columns)
    toeplitz, enter, leave, powers, taps = mats
    gated = pl.pallas_call(
        conv_body,
        out_shape=pltpu.VMEM((2 * shards, owned, tokens), bf16),
        in_specs=[in_vmem] * 6,
        out_specs=in_vmem,
        scratch_shapes=[pltpu.VMEM((blocks, owned, LANES), f32)] * 3,
        cost_estimate=pl.CostEstimate(flops=WAIT, bytes_accessed=2500000, transcendentals=0),
        compiler_params=params(),
        name="conv",
    )(*map(near, (held, taps, toeplitz, enter, leave, powers)))
    gated = pl.pallas_call(
        hold_body,
        out_shape=pltpu.VMEM((2 * shards, owned, tokens), bf16),
        in_specs=[in_vmem] + [pl.BlockSpec(memory_space=pl.ANY)] * 3,
        out_specs=in_vmem,
        compiler_params=params(),
        name="hold",
    )(near(gated), *(weights[d] for d in ORDER))
    gated = exchange(gated, BACK)
    gated = pl.pallas_call(
        settle_body,
        out_shape=pltpu.VMEM((2 * channels, tokens), bf16),
        in_specs=[in_vmem],
        out_specs=in_vmem,
        compiler_params=params(),
        name="settle",
    )(near(gated))
    other = shift(gated, "c", 1)
    rows = out_weight.shape[0]
    one = core.reshape(1)
    close = [near(w) for w in weights]
    sums = pl.pallas_call(
        own_body,
        out_shape=(pltpu.VMEM((rows, tokens), f32),) * 4,
        in_specs=[pl.BlockSpec(memory_space=pltpu.SMEM)] + [in_vmem] * 5,
        out_specs=(in_vmem,) * 4,
        cost_estimate=pl.CostEstimate(flops=150000000, bytes_accessed=1500000, transcendentals=0),
        compiler_params=params(),
        name="own",
    )(one, near(gated), *close)
    parts = pl.pallas_call(
        other_body,
        out_shape=(pltpu.VMEM((rows, tokens), f32),) + (pltpu.VMEM((rows, tokens), bf16),) * 3,
        in_specs=[pl.BlockSpec(memory_space=pltpu.SMEM)] + [in_vmem] * 9,
        out_specs=(in_vmem,) * 4,
        cost_estimate=pl.CostEstimate(flops=150000000, bytes_accessed=1500000, transcendentals=0),
        compiler_params=params(),
        name="other",
    )(one, near(other), *close, *map(near, sums))
    arrived = [parts[0]] + [shift(parts[d], "y", d) for d in (2, 1, 3)]
    return pl.pallas_call(
        add_body,
        out_shape=jax.ShapeDtypeStruct((rows, tokens), bf16),
        in_specs=[in_vmem] * 4,
        out_specs=in_vmem,
        compiler_params=params(),
        name="add",
    )(*map(near, arrived))


def solution(mesh):
    split = Mesh(mesh.devices.reshape(4, 4, 4, 2, 2), CTX + CH)
    in_specs = (
        P(None, CH, CTX),
        P(None, CH, None),
        P(CH + CTX, None),
        P(CH + CTX, None),
        P(CH),
        P(CH, None),
    )
    return jax.shard_map(local, mesh=split, in_specs=in_specs, out_specs=P(CH, CTX), check_vma=False)
```

```python
import jax
import jax.numpy as jnp
from jax import lax
from jax.experimental import pallas as pl
from jax.experimental.pallas import tpu as pltpu
from jax.sharding import Mesh
from jax.sharding import PartitionSpec as P

CTX = ("x", "zl")
CH = ("y", "zh", "c")
GO = ("zl", "x")
BACK = ("zl", "x", "zh")
LANES = 128
TAPS = 3
TURN = {16: (8, 4), 32: (20, 12)}
ORDER = (2, 1, 3)
WAIT = 20_000_000_000
f32 = jnp.float32
bf16 = jnp.bfloat16
in_vmem = pl.BlockSpec(memory_space=pltpu.VMEM)


def shift(value, axis, steps):
    count = lax.axis_size(axis)
    return lax.ppermute(value, axis, [(i, (i + steps) % count) for i in range(count)])


def place(order, k, h=0):
    at = {"x": k // 4, "zl": k % 4, "zh": h}
    size = {"x": 4, "zl": 4, "zh": 2}
    index, count = 0, 1
    for axis in order:
        index = index * size[axis] + at[axis]
        count *= size[axis]
    return count - 1 - index


def spot(order, k, h=0):
    count = 4 ** 2 * (2 if "zh" in order else 1)
    first, second = TURN[count]
    turned = jnp.where(lax.axis_index("c") == 0, count - first, count - second)
    return lax.rem(place(order, k, h) + turned, count)


def exchange(value, order):
    count = value.shape[0]
    groups = [
        [2 * (count - 1 - (i + TURN[count][c]) % count) + c for i in range(count)] for c in (0, 1)
    ]
    return lax.all_to_all(value, order + ("c",), 0, 0, axis_index_groups=groups, tiled=True)


def near(value):
    return pltpu.with_memory_space_constraint(value, pltpu.VMEM)


def params(**kwargs):
    return pltpu.CompilerParams(vmem_limit_bytes=16 << 20, **kwargs)


def ctx_index():
    return lax.axis_index("x") * lax.axis_size("zl") + lax.axis_index("zl")


def split(value):
    high = value.astype(bf16)
    return high, (value - high.astype(f32)).astype(bf16)


def pack_body(features_hbm, taps_hbm, sent, features, short_taps, sem):
    copies = [pltpu.make_async_copy(taps_hbm, short_taps, sem.at[3])]
    for s in range(3):
        copies.append(pltpu.make_async_copy(features_hbm.at[s], features.at[s], sem.at[s]))
    for copy in copies:
        copy.start()
    for copy in copies:
        copy.wait()
    _, channels, tokens = features.shape
    shards, owned, _ = sent.shape
    per = tokens // LANES
    rows = [short_taps[s] for s in range(3)]
    filler = jnp.zeros((LANES - 3 * TAPS, channels), f32)
    columns = jnp.transpose(jnp.concatenate(rows + [filler], axis=0))
    lane = lax.broadcasted_iota(jnp.int32, (owned, LANES), 1)
    zero = jnp.zeros((owned, LANES), f32)
    for k in range(shards):
        at = slice(k * owned, (k + 1) * owned)
        rims = zero
        value = [[], [], []]
        for s in range(3):
            w = [
                jnp.broadcast_to(columns[at, i : i + 1], (owned, LANES))
                for i in range(s * TAPS, (s + 1) * TAPS)
            ]
            last = (zero, zero)
            for j in range(per):
                now = features[s, at, j * LANES : (j + 1) * LANES].astype(f32)
                one, two = pltpu.roll(now, 1, 1), pltpu.roll(now, 2, 1)
                value[s].append(
                    w[0] * now
                    + w[1] * jnp.where(lane < 1, last[0], one)
                    + w[2] * jnp.where(lane < 2, last[1], two)
                )
                last = (one, two)
                if j == 0:
                    head = pltpu.roll(now, 4 * s, 1) if s else now
                    rims = jnp.where((lane == 4 * s) | (lane == 4 * s + 1), head, rims)
                if j == per - 1:
                    tail = pltpu.roll(now, 4 * s + 4, 1)
                    rims = jnp.where((lane == 4 * s + 2) | (lane == 4 * s + 3), tail, rims)
        for j in range(per):
            part = slice(j * LANES, (j + 1) * LANES)
            sent[spot(GO, k), :, part] = (value[1][j] * value[2][j]).astype(bf16)
            part = slice(tokens + j * LANES, tokens + (j + 1) * LANES)
            sent[spot(GO, k), :, part] = value[0][j].astype(bf16)
        sent[spot(GO, k), :, 2 * tokens :] = rims.astype(bf16)


def prep_body(decay, residue, skip_bias, short_taps, toeplitz, enter, leave, powers, taps):
    owned, modes = decay.shape
    lane = lax.broadcasted_iota(jnp.int32, (owned, LANES), 1)
    sub = lax.broadcasted_iota(jnp.int32, (owned, LANES), 0)
    mine = lane == sub + ctx_index() * owned

    def own_column(values):
        picked = jnp.sum(jnp.where(mine, values, 0.0), axis=1, keepdims=True)
        return jnp.broadcast_to(picked, (owned, LANES))

    def as_row(values):
        tiled = jnp.concatenate([values] * owned, axis=1)
        return jnp.sum(jnp.where(lane // modes == sub, tiled, 0.0), axis=0, keepdims=True)

    for s in range(3):
        for j in range(TAPS):
            taps[s * TAPS + j] = own_column(short_taps[s, j : j + 1, :])
    moment = lane.astype(f32)
    impulse = jnp.where(lane == 0, own_column(skip_bias[...]), 0.0)
    rates, weights = decay[...], residue[...]
    for n in range(modes):
        impulse = impulse + weights[:, n : n + 1] * jnp.exp(-rates[:, n : n + 1] * moment)
    row = lax.broadcasted_iota(jnp.int32, (LANES, LANES), 0)
    col = lax.broadcasted_iota(jnp.int32, (LANES, LANES), 1)
    rate = as_row(rates)
    into = jnp.exp(-rate * (LANES - 1 - row).astype(f32))
    out_of = jnp.transpose(as_row(weights) * jnp.exp(-rate * (row + 1).astype(f32)))
    for c in range(owned):
        spread = jnp.broadcast_to(impulse[c : c + 1, :], (LANES, LANES))
        rolled = pltpu.roll(spread, 0, 1, stride=1, stride_axis=0)
        high, low = split(jnp.where(col >= row, rolled, 0.0))
        toeplitz[c, :LANES, :] = high
        toeplitz[c, LANES:, :] = low
        part = slice(c * LANES, (c + 1) * LANES)
        high, low = split(jnp.where(col // modes == c, into, 0.0))
        enter[part, :LANES] = high
        enter[part, LANES:] = low
        high, low = split(jnp.where(row // modes == c, out_of, 0.0))
        leave[:LANES, part] = high
        leave[LANES : 2 * LANES, part] = high
        leave[2 * LANES :, part] = low
    for i in range(8):
        powers[i : i + 1, :] = jnp.exp(-rate * float(LANES << i))


def dot(a, b):
    return jnp.dot(a, b, preferred_element_type=f32)


def conv_body(held, taps, toeplitz, enter, leave, powers, out, mixed_buf, query_buf, conv_buf):
    shards, owned, _ = held.shape
    tokens = out.shape[-1]
    per = tokens // LANES
    blocks = shards * per
    lane = lax.broadcasted_iota(jnp.int32, (owned, LANES), 1)
    weights = [
        jnp.where(lane < 4, taps[j], jnp.where(lane < 8, taps[TAPS + j], taps[2 * TAPS + j]))
        for j in range(TAPS)
    ]
    before = jnp.zeros((owned, LANES), f32)
    for k in range(shards):
        rims = held[spot(GO, k), :, 2 * tokens :].astype(f32)
        older = pltpu.roll(before, LANES - 2, 1)
        middle = jnp.where(lane % 4 == 0, pltpu.roll(before, LANES - 3, 1), pltpu.roll(rims, 1, 1))
        head = weights[0] * rims + weights[1] * middle + weights[2] * older
        before = rims
        fixed = pltpu.roll(head, LANES - 4, 1) * pltpu.roll(head, LANES - 8, 1)
        for j in range(per):
            now = held[spot(GO, k), :, j * LANES : (j + 1) * LANES].astype(f32)
            query = held[spot(GO, k), :, tokens + j * LANES : tokens + (j + 1) * LANES].astype(f32)
            if j == 0:
                now = jnp.where(lane < 2, fixed.astype(bf16).astype(f32), now)
                query = jnp.where(lane < 2, head, query)
            mixed_buf[k * per + j] = now
            query_buf[k * per + j] = query
    mixed = [mixed_buf[:, c, :].astype(bf16) for c in range(owned)]
    whole = jnp.concatenate(mixed, axis=1)
    state = dot(whole, enter[...])
    state = state[:, :LANES] + state[:, LANES:]
    row = lax.broadcasted_iota(jnp.int32, (blocks, LANES), 0)
    step, i = 1, 0
    while step < blocks:
        moved = jnp.where(row < step, 0.0, pltpu.roll(state, step, 0))
        state = state + powers[i : i + 1, :] * moved
        step, i = step * 2, i + 1
    state = jnp.where(row < 1, 0.0, pltpu.roll(state, 1, 0))
    high, low = split(state)
    carried = dot(jnp.concatenate([high, low, high], axis=1), leave[...])
    for c in range(owned):
        value = dot(jnp.concatenate([mixed[c], mixed[c]], axis=1), toeplitz[c])
        conv_buf[:, c, :] = value + carried[:, c * LANES : (c + 1) * LANES]
    for b in range(blocks):
        k, j = divmod(b, per)
        value = (query_buf[b] * conv_buf[b]).astype(bf16)
        for h in range(2):
            out[spot(BACK, k, h), :, j * LANES : (j + 1) * LANES] = value


def hold_body(gated, w1, w2, w3, out):
    out[...] = gated[...]


def settle_body(gated, out):
    count, owned, _ = gated.shape
    for h in range(2):
        rows = [gated[spot(BACK, k, h)] for k in range(count // 2)]
        out[pl.ds(h * (count // 2) * owned, count // 2 * owned), :] = jnp.concatenate(rows, axis=0)


def columns_of(w, core, half):
    return [w[:, pl.ds(pl.multiple_of((2 * h + core) * half, half), half)] for h in range(2)]


def own_body(core, own, w0, w1, w2, w3, o0, o1, o2, o3):
    half = own.shape[0] // 2
    for w, o in ((w0, o0), (w1, o1), (w2, o2), (w3, o3)):
        o[...] = dot(jnp.concatenate(columns_of(w, core[0], half), axis=1), own[...])


def other_body(core, other, w0, w1, w2, w3, a0, a1, a2, a3, o0, o1, o2, o3):
    half = other.shape[0] // 2
    for w, a, o in ((w2, a2, o2), (w1, a1, o1), (w3, a3, o3), (w0, a0, o0)):
        term = dot(jnp.concatenate(columns_of(w, 1 - core[0], half), axis=1), other[...])
        o[...] = (a[...] + term).astype(o.dtype)


def add_body(o0, o1, o2, o3, out):
    total = o0[...] + o1[...].astype(f32) + o2[...].astype(f32) + o3[...].astype(f32)
    out[...] = total.astype(out.dtype)


def local(features, short_taps, decay, residue, skip_bias, out_weight):
    _, channels, tokens = features.shape
    shards = lax.axis_size("x") * lax.axis_size("zl")
    owned, modes = decay.shape
    blocks = shards * tokens // LANES
    y, zh, core = (lax.axis_index(a) for a in CH)

    columns = short_taps.transpose(0, 2, 1)
    sent = pl.pallas_call(
        pack_body,
        out_shape=pltpu.VMEM((shards, owned, 2 * tokens + LANES), bf16),
        in_specs=[pl.BlockSpec(memory_space=pltpu.HBM)] * 2,
        out_specs=in_vmem,
        scratch_shapes=[
            pltpu.VMEM(features.shape, bf16),
            pltpu.VMEM(columns.shape, f32),
            pltpu.SemaphoreType.DMA((4,)),
        ],
        compiler_params=params(),
        name="pack",
    )(*(pltpu.with_memory_space_constraint(a, pltpu.HBM) for a in (features, columns)))
    held = exchange(sent, GO)

    ys = lax.axis_size("y")
    cols = out_weight.shape[1] // ys
    weights = {0: lax.dynamic_slice_in_dim(out_weight, y * cols, cols, 1)}
    for d in ORDER:
        block = lax.dynamic_slice_in_dim(out_weight, (y + ys - d) % ys * cols, cols, 1)
        weights[d] = shift(block, "y", -d)
    weights = [weights[d] for d in range(ys)]

    mats = pl.pallas_call(
        prep_body,
        out_shape=(
            pltpu.VMEM((owned, 2 * LANES, LANES), bf16),
            pltpu.VMEM((owned * LANES, 2 * LANES), bf16),
            pltpu.VMEM((3 * LANES, owned * LANES), bf16),
            pltpu.VMEM((8, LANES), f32),
            pltpu.VMEM((3 * TAPS, owned, LANES), f32),
        ),
        in_specs=[in_vmem] * 4,
        out_specs=(in_vmem,) * 5,
        cost_estimate=pl.CostEstimate(flops=2000000, bytes_accessed=1600000, transcendentals=70000),
        compiler_params=params(),
        name="prep",
    )(decay, residue, skip_bias.reshape(1, -1), columns)
    toeplitz, enter, leave, powers, taps = mats
    gated = pl.pallas_call(
        conv_body,
        out_shape=pltpu.VMEM((2 * shards, owned, tokens), bf16),
        in_specs=[in_vmem] * 6,
        out_specs=in_vmem,
        scratch_shapes=[pltpu.VMEM((blocks, owned, LANES), f32)] * 3,
        cost_estimate=pl.CostEstimate(flops=WAIT, bytes_accessed=2500000, transcendentals=0),
        compiler_params=params(),
        name="conv",
    )(*map(near, (held, taps, toeplitz, enter, leave, powers)))
    gated = pl.pallas_call(
        hold_body,
        out_shape=pltpu.VMEM((2 * shards, owned, tokens), bf16),
        in_specs=[in_vmem] + [pl.BlockSpec(memory_space=pl.ANY)] * 3,
        out_specs=in_vmem,
        compiler_params=params(),
        name="hold",
    )(near(gated), *(weights[d] for d in ORDER))
    gated = exchange(gated, BACK)
    gated = pl.pallas_call(
        settle_body,
        out_shape=pltpu.VMEM((2 * channels, tokens), bf16),
        in_specs=[in_vmem],
        out_specs=in_vmem,
        compiler_params=params(),
        name="settle",
    )(near(gated))
    other = shift(gated, "c", 1)
    rows = out_weight.shape[0]
    one = core.reshape(1)
    close = [near(w) for w in weights]
    sums = pl.pallas_call(
        own_body,
        out_shape=(pltpu.VMEM((rows, tokens), f32),) * 4,
        in_specs=[pl.BlockSpec(memory_space=pltpu.SMEM)] + [in_vmem] * 5,
        out_specs=(in_vmem,) * 4,
        cost_estimate=pl.CostEstimate(flops=150000000, bytes_accessed=1500000, transcendentals=0),
        compiler_params=params(),
        name="own",
    )(one, near(gated), *close)
    parts = pl.pallas_call(
        other_body,
        out_shape=(pltpu.VMEM((rows, tokens), f32),) + (pltpu.VMEM((rows, tokens), bf16),) * 3,
        in_specs=[pl.BlockSpec(memory_space=pltpu.SMEM)] + [in_vmem] * 9,
        out_specs=(in_vmem,) * 4,
        cost_estimate=pl.CostEstimate(flops=150000000, bytes_accessed=1500000, transcendentals=0),
        compiler_params=params(),
        name="other",
    )(one, near(other), *close, *map(near, sums))
    arrived = [parts[0]] + [shift(parts[d], "y", d) for d in (2, 1, 3)]
    return pl.pallas_call(
        add_body,
        out_shape=jax.ShapeDtypeStruct((rows, tokens), bf16),
        in_specs=[in_vmem] * 4,
        out_specs=in_vmem,
        compiler_params=params(),
        name="add",
    )(*map(near, arrived))


def solution(mesh):
    split = Mesh(mesh.devices.reshape(4, 4, 4, 2, 2), CTX + CH)
    in_specs = (
        P(None, CH, CTX),
        P(None, CH, None),
        P(CH + CTX, None),
        P(CH + CTX, None),
        P(CH),
        P(CH, None),
    )
    return jax.shard_map(local, mesh=split, in_specs=in_specs, out_specs=P(CH, CTX), check_vma=False)
```

```python
import jax
import jax.numpy as jnp
from jax import lax
from jax.experimental import pallas as pl
from jax.experimental.pallas import tpu as pltpu
from jax.sharding import Mesh
from jax.sharding import PartitionSpec as P

CTX = ("x", "zl")
CH = ("y", "zh", "c")
GO = ("zl", "x")
BACK = ("zl", "x", "zh")
LANES = 128
TAPS = 3
TURN = {16: (8, 4), 32: (20, 12)}
ORDER = (2, 1, 3)
WAIT = 20_000_000_000
f32 = jnp.float32
bf16 = jnp.bfloat16
in_vmem = pl.BlockSpec(memory_space=pltpu.VMEM)


def shift(value, axis, steps):
    count = lax.axis_size(axis)
    return lax.ppermute(value, axis, [(i, (i + steps) % count) for i in range(count)])


def place(order, k, h=0):
    at = {"x": k // 4, "zl": k % 4, "zh": h}
    size = {"x": 4, "zl": 4, "zh": 2}
    index, count = 0, 1
    for axis in order:
        index = index * size[axis] + at[axis]
        count *= size[axis]
    return count - 1 - index


def spot(order, k, h=0):
    count = 4 ** 2 * (2 if "zh" in order else 1)
    first, second = TURN[count]
    turned = jnp.where(lax.axis_index("c") == 0, count - first, count - second)
    return lax.rem(place(order, k, h) + turned, count)


def exchange(value, order):
    count = value.shape[0]
    groups = [
        [2 * (count - 1 - (i + TURN[count][c]) % count) + c for i in range(count)] for c in (0, 1)
    ]
    return lax.all_to_all(value, order + ("c",), 0, 0, axis_index_groups=groups, tiled=True)


def near(value):
    return pltpu.with_memory_space_constraint(value, pltpu.VMEM)


def params(**kwargs):
    return pltpu.CompilerParams(vmem_limit_bytes=16 << 20, **kwargs)


def ctx_index():
    return lax.axis_index("x") * lax.axis_size("zl") + lax.axis_index("zl")


def split(value):
    high = value.astype(bf16)
    return high, (value - high.astype(f32)).astype(bf16)


def pack_body(features_hbm, taps_hbm, sent, features, short_taps, sem):
    copies = [pltpu.make_async_copy(taps_hbm, short_taps, sem.at[3])]
    for s in range(3):
        copies.append(pltpu.make_async_copy(features_hbm.at[s], features.at[s], sem.at[s]))
    for copy in copies:
        copy.start()
    for copy in copies:
        copy.wait()
    _, channels, tokens = features.shape
    shards, owned, _ = sent.shape
    per = tokens // LANES
    rows = [short_taps[s] for s in range(3)]
    filler = jnp.zeros((LANES - 3 * TAPS, channels), f32)
    columns = jnp.transpose(jnp.concatenate(rows + [filler], axis=0))
    lane = lax.broadcasted_iota(jnp.int32, (owned, LANES), 1)
    zero = jnp.zeros((owned, LANES), f32)
    for k in range(shards):
        at = slice(k * owned, (k + 1) * owned)
        rims = zero
        value = [[], [], []]
        for s in range(3):
            w = [
                jnp.broadcast_to(columns[at, i : i + 1], (owned, LANES))
                for i in range(s * TAPS, (s + 1) * TAPS)
            ]
            last = (zero, zero)
            for j in range(per):
                now = features[s, at, j * LANES : (j + 1) * LANES].astype(f32)
                one, two = pltpu.roll(now, 1, 1), pltpu.roll(now, 2, 1)
                value[s].append(
                    w[0] * now
                    + w[1] * jnp.where(lane < 1, last[0], one)
                    + w[2] * jnp.where(lane < 2, last[1], two)
                )
                last = (one, two)
                if j == 0:
                    head = pltpu.roll(now, 4 * s, 1) if s else now
                    rims = jnp.where((lane == 4 * s) | (lane == 4 * s + 1), head, rims)
                if j == per - 1:
                    tail = pltpu.roll(now, 4 * s + 4, 1)
                    rims = jnp.where((lane == 4 * s + 2) | (lane == 4 * s + 3), tail, rims)
        for j in range(per):
            part = slice(j * LANES, (j + 1) * LANES)
            sent[spot(GO, k), :, part] = (value[1][j] * value[2][j]).astype(bf16)
            part = slice(tokens + j * LANES, tokens + (j + 1) * LANES)
            sent[spot(GO, k), :, part] = value[0][j].astype(bf16)
        sent[spot(GO, k), :, 2 * tokens :] = rims.astype(bf16)


def prep_body(decay, residue, skip_bias, short_taps, toeplitz, enter, leave, powers, taps):
    owned, modes = decay.shape
    lane = lax.broadcasted_iota(jnp.int32, (owned, LANES), 1)
    sub = lax.broadcasted_iota(jnp.int32, (owned, LANES), 0)
    mine = lane == sub + ctx_index() * owned

    def own_column(values):
        picked = jnp.sum(jnp.where(mine, values, 0.0), axis=1, keepdims=True)
        return jnp.broadcast_to(picked, (owned, LANES))

    def as_row(values):
        tiled = jnp.concatenate([values] * owned, axis=1)
        return jnp.sum(jnp.where(lane // modes == sub, tiled, 0.0), axis=0, keepdims=True)

    for s in range(3):
        for j in range(TAPS):
            taps[s * TAPS + j] = own_column(short_taps[s, j : j + 1, :])
    moment = lane.astype(f32)
    impulse = jnp.where(lane == 0, own_column(skip_bias[...]), 0.0)
    rates, weights = decay[...], residue[...]
    for n in range(modes):
        impulse = impulse + weights[:, n : n + 1] * jnp.exp(-rates[:, n : n + 1] * moment)
    row = lax.broadcasted_iota(jnp.int32, (LANES, LANES), 0)
    col = lax.broadcasted_iota(jnp.int32, (LANES, LANES), 1)
    rate = as_row(rates)
    into = jnp.exp(-rate * (LANES - 1 - row).astype(f32))
    out_of = jnp.transpose(as_row(weights) * jnp.exp(-rate * (row + 1).astype(f32)))
    for c in range(owned):
        spread = jnp.broadcast_to(impulse[c : c + 1, :], (LANES, LANES))
        rolled = pltpu.roll(spread, 0, 1, stride=1, stride_axis=0)
        high, low = split(jnp.where(col >= row, rolled, 0.0))
        toeplitz[c, :LANES, :] = high
        toeplitz[c, LANES:, :] = low
        part = slice(c * LANES, (c + 1) * LANES)
        high, low = split(jnp.where(col // modes == c, into, 0.0))
        enter[part, :LANES] = high
        enter[part, LANES:] = low
        high, low = split(jnp.where(row // modes == c, out_of, 0.0))
        leave[:LANES, part] = high
        leave[LANES : 2 * LANES, part] = high
        leave[2 * LANES :, part] = low
    for i in range(8):
        powers[i : i + 1, :] = jnp.exp(-rate * float(LANES << i))


def dot(a, b):
    return jnp.dot(a, b, preferred_element_type=f32)


def conv_body(held, taps, toeplitz, enter, leave, powers, out, mixed_buf, query_buf, conv_buf):
    shards, owned, _ = held.shape
    tokens = out.shape[-1]
    per = tokens // LANES
    blocks = shards * per
    lane = lax.broadcasted_iota(jnp.int32, (owned, LANES), 1)
    weights = [
        jnp.where(lane < 4, taps[j], jnp.where(lane < 8, taps[TAPS + j], taps[2 * TAPS + j]))
        for j in range(TAPS)
    ]
    before = jnp.zeros((owned, LANES), f32)
    for k in range(shards):
        rims = held[spot(GO, k), :, 2 * tokens :].astype(f32)
        older = pltpu.roll(before, LANES - 2, 1)
        middle = jnp.where(lane % 4 == 0, pltpu.roll(before, LANES - 3, 1), pltpu.roll(rims, 1, 1))
        head = weights[0] * rims + weights[1] * middle + weights[2] * older
        before = rims
        fixed = pltpu.roll(head, LANES - 4, 1) * pltpu.roll(head, LANES - 8, 1)
        for j in range(per):
            now = held[spot(GO, k), :, j * LANES : (j + 1) * LANES].astype(f32)
            query = held[spot(GO, k), :, tokens + j * LANES : tokens + (j + 1) * LANES].astype(f32)
            if j == 0:
                now = jnp.where(lane < 2, fixed.astype(bf16).astype(f32), now)
                query = jnp.where(lane < 2, head, query)
            mixed_buf[k * per + j] = now
            query_buf[k * per + j] = query
    mixed = [mixed_buf[:, c, :].astype(bf16) for c in range(owned)]
    whole = jnp.concatenate(mixed, axis=1)
    state = dot(whole, enter[...])
    state = state[:, :LANES] + state[:, LANES:]
    row = lax.broadcasted_iota(jnp.int32, (blocks, LANES), 0)
    step, i = 1, 0
    while step < blocks:
        moved = jnp.where(row < step, 0.0, pltpu.roll(state, step, 0))
        state = state + powers[i : i + 1, :] * moved
        step, i = step * 2, i + 1
    state = jnp.where(row < 1, 0.0, pltpu.roll(state, 1, 0))
    high, low = split(state)
    carried = dot(jnp.concatenate([high, low, high], axis=1), leave[...])
    for c in range(owned):
        value = dot(jnp.concatenate([mixed[c], mixed[c]], axis=1), toeplitz[c])
        conv_buf[:, c, :] = value + carried[:, c * LANES : (c + 1) * LANES]
    for b in range(blocks):
        k, j = divmod(b, per)
        value = (query_buf[b] * conv_buf[b]).astype(bf16)
        for h in range(2):
            out[spot(BACK, k, h), :, j * LANES : (j + 1) * LANES] = value


def hold_body(gated, w1, w2, w3, out):
    out[...] = gated[...]


def settle_body(gated, out):
    count, owned, _ = gated.shape
    for h in range(2):
        rows = [gated[spot(BACK, k, h)] for k in range(count // 2)]
        out[pl.ds(h * (count // 2) * owned, count // 2 * owned), :] = jnp.concatenate(rows, axis=0)


def columns_of(w, core, half):
    return [w[:, pl.ds(pl.multiple_of((2 * h + core) * half, half), half)] for h in range(2)]


def own_body(core, own, w0, w1, w2, w3, o0, o1, o2, o3):
    half = own.shape[0] // 2
    for w, o in ((w0, o0), (w1, o1), (w2, o2), (w3, o3)):
        o[...] = dot(jnp.concatenate(columns_of(w, core[0], half), axis=1), own[...])


def other_body(core, other, w1, w2, w3, a1, a2, a3, o1, o2, o3):
    half = other.shape[0] // 2
    for w, a, o in ((w2, a2, o2), (w1, a1, o1), (w3, a3, o3)):
        term = dot(jnp.concatenate(columns_of(w, 1 - core[0], half), axis=1), other[...])
        o[...] = (a[...] + term).astype(o.dtype)


def home_body(core, other, w0, a0, o0):
    half = other.shape[0] // 2
    term = dot(jnp.concatenate(columns_of(w0, 1 - core[0], half), axis=1), other[...])
    o0[...] = a0[...] + term


def add_body(o0, o1, o2, o3, out):
    total = o0[...] + o1[...].astype(f32) + o2[...].astype(f32) + o3[...].astype(f32)
    out[...] = total.astype(out.dtype)


def local(features, short_taps, decay, residue, skip_bias, out_weight):
    _, channels, tokens = features.shape
    shards = lax.axis_size("x") * lax.axis_size("zl")
    owned, modes = decay.shape
    blocks = shards * tokens // LANES
    y, zh, core = (lax.axis_index(a) for a in CH)

    columns = short_taps.transpose(0, 2, 1)
    sent = pl.pallas_call(
        pack_body,
        out_shape=pltpu.VMEM((shards, owned, 2 * tokens + LANES), bf16),
        in_specs=[pl.BlockSpec(memory_space=pltpu.HBM)] * 2,
        out_specs=in_vmem,
        scratch_shapes=[
            pltpu.VMEM(features.shape, bf16),
            pltpu.VMEM(columns.shape, f32),
            pltpu.SemaphoreType.DMA((4,)),
        ],
        compiler_params=params(),
        name="pack",
    )(*(pltpu.with_memory_space_constraint(a, pltpu.HBM) for a in (features, columns)))
    held = exchange(sent, GO)

    ys = lax.axis_size("y")
    cols = out_weight.shape[1] // ys
    weights = {0: lax.dynamic_slice_in_dim(out_weight, y * cols, cols, 1)}
    for d in ORDER:
        block = lax.dynamic_slice_in_dim(out_weight, (y + ys - d) % ys * cols, cols, 1)
        weights[d] = shift(block, "y", -d)
    weights = [weights[d] for d in range(ys)]

    mats = pl.pallas_call(
        prep_body,
        out_shape=(
            pltpu.VMEM((owned, 2 * LANES, LANES), bf16),
            pltpu.VMEM((owned * LANES, 2 * LANES), bf16),
            pltpu.VMEM((3 * LANES, owned * LANES), bf16),
            pltpu.VMEM((8, LANES), f32),
            pltpu.VMEM((3 * TAPS, owned, LANES), f32),
        ),
        in_specs=[in_vmem] * 4,
        out_specs=(in_vmem,) * 5,
        cost_estimate=pl.CostEstimate(flops=2000000, bytes_accessed=1600000, transcendentals=70000),
        compiler_params=params(),
        name="prep",
    )(decay, residue, skip_bias.reshape(1, -1), columns)
    toeplitz, enter, leave, powers, taps = mats
    gated = pl.pallas_call(
        conv_body,
        out_shape=pltpu.VMEM((2 * shards, owned, tokens), bf16),
        in_specs=[in_vmem] * 6,
        out_specs=in_vmem,
        scratch_shapes=[pltpu.VMEM((blocks, owned, LANES), f32)] * 3,
        cost_estimate=pl.CostEstimate(flops=WAIT, bytes_accessed=2500000, transcendentals=0),
        compiler_params=params(),
        name="conv",
    )(*map(near, (held, taps, toeplitz, enter, leave, powers)))
    gated = pl.pallas_call(
        hold_body,
        out_shape=pltpu.VMEM((2 * shards, owned, tokens), bf16),
        in_specs=[in_vmem] + [pl.BlockSpec(memory_space=pl.ANY)] * 3,
        out_specs=in_vmem,
        compiler_params=params(),
        name="hold",
    )(near(gated), *(weights[d] for d in ORDER))
    gated = exchange(gated, BACK)
    gated = pl.pallas_call(
        settle_body,
        out_shape=pltpu.VMEM((2 * channels, tokens), bf16),
        in_specs=[in_vmem],
        out_specs=in_vmem,
        compiler_params=params(),
        name="settle",
    )(near(gated))
    other = shift(gated, "c", 1)
    rows = out_weight.shape[0]
    one = core.reshape(1)
    close = [near(w) for w in weights]
    sums = pl.pallas_call(
        own_body,
        out_shape=(pltpu.VMEM((rows, tokens), f32),) * 4,
        in_specs=[pl.BlockSpec(memory_space=pltpu.SMEM)] + [in_vmem] * 5,
        out_specs=(in_vmem,) * 4,
        cost_estimate=pl.CostEstimate(flops=150000000, bytes_accessed=1500000, transcendentals=0),
        compiler_params=params(),
        name="own",
    )(one, near(gated), *close)
    parts = pl.pallas_call(
        other_body,
        out_shape=(pltpu.VMEM((rows, tokens), bf16),) * 3,
        in_specs=[pl.BlockSpec(memory_space=pltpu.SMEM)] + [in_vmem] * 7,
        out_specs=(in_vmem,) * 3,
        cost_estimate=pl.CostEstimate(flops=110000000, bytes_accessed=1500000, transcendentals=0),
        compiler_params=params(),
        name="other",
    )(one, near(other), *close[1:], *map(near, sums[1:]))
    home = pl.pallas_call(
        home_body,
        out_shape=pltpu.VMEM((rows, tokens), f32),
        in_specs=[pl.BlockSpec(memory_space=pltpu.SMEM)] + [in_vmem] * 3,
        out_specs=in_vmem,
        cost_estimate=pl.CostEstimate(flops=40000000, bytes_accessed=500000, transcendentals=0),
        compiler_params=params(),
        name="home",
    )(one, near(other), close[0], near(sums[0]))
    parts = (home,) + tuple(parts)
    arrived = [parts[0]] + [shift(parts[d], "y", d) for d in (2, 1, 3)]
    return pl.pallas_call(
        add_body,
        out_shape=jax.ShapeDtypeStruct((rows, tokens), bf16),
        in_specs=[in_vmem] * 4,
        out_specs=in_vmem,
        compiler_params=params(),
        name="add",
    )(*map(near, arrived))


def solution(mesh):
    split = Mesh(mesh.devices.reshape(4, 4, 4, 2, 2), CTX + CH)
    in_specs = (
        P(None, CH, CTX),
        P(None, CH, None),
        P(CH + CTX, None),
        P(CH + CTX, None),
        P(CH),
        P(CH, None),
    )
    return jax.shard_map(local, mesh=split, in_specs=in_specs, out_specs=P(CH, CTX), check_vma=False)
```
